512 devices in a mesh: light: 4 (over x_lo, core), strip: 128 (over z, y, x_hi).
Axes of the slice: x: 4 (x_hi: 2, x_lo: 2; x = x_hi * 2 + x_lo), y: 8, z: 8, core: 2. Of those that a mesh axis runs over, the one named last changes fastest.
Arguments:
- depth_start: float32 [128, 65536], P(None, 'strip'), may hold values from -0.3 to 0.3
- albedo_start: float32 [128, 65536], P(None, 'strip'), may hold values from 0.5 to 2
- observations: bfloat16 [32, 128, 65536], P('light', None, 'strip'), may hold values from 0 to 26
- light_table: int32 [32, 4], P('light'), may hold values from 0 to 999
- valid_mask: int32 [128, 65536], P(None, 'strip'), may hold values 0 or 1
Outputs:
- depth_final: float32 [128, 65536], P(None, 'strip')
- albedo_final: float32 [128, 65536], P(None, 'strip')
The draws below stay inside these ranges and needn't reach their ends.
All inputs are finite; a program needn't handle non-finite values. No bound on the sum of `valid_mask` on one device may be relied on, other than what follows from the above.
Results may differ from the reference program's by a relative error of at most 0.0003.
Values may be sent and summed in bfloat16 or wider, within the bound.
A program may use at most 64 MiB of HBM per device.

```python
import math
import jax
import jax.numpy as jnp
from jax import lax

NL = 32
ROWS = 128
ITERS = 2
COLS = 65536


def draw_observations(key, part):
    subkeys = jax.random.split(key, 3)
    row_scale = jnp.exp(jax.random.uniform(subkeys[0], (1, ROWS, 1), jnp.float32, 0.0, math.log(1.6)))
    col_scale = jnp.exp(jax.random.uniform(subkeys[1], (1, 1, COLS), jnp.float32, 0.0, math.log(1.6)))
    position = jnp.arange(COLS, dtype=jnp.float32) / max(COLS - 1, 1)
    incline = (1.0 + 8.0 * position)[None, None, :]
    texture = jax.random.uniform(subkeys[2], (NL, ROWS, COLS), jnp.float32, 0.2, 1.1)
    values = row_scale * col_scale * incline * texture
    return values.astype(jnp.bfloat16)


def plant(result, own_key, least, high):
    longest = result.shape.index(max(result.shape))
    spots = []
    for shift in (0, 1):
        where = [jax.random.randint(jax.random.fold_in(own_key, axis), (), 0, length) for axis, length in enumerate(result.shape)]
        where[longest] = (where[longest] + shift) % result.shape[longest]
        spots.append(tuple(where))
    return result.at[spots[0]].set(least).at[spots[1]].set(high)


def block_levels(stream_key, dims, pieces, low, high):
    level, own = 1.0, jax.random.fold_in(stream_key, 6)
    for dim, shards_of in pieces:
        draws = jnp.exp(jax.random.uniform(jax.random.fold_in(own, dim), (shards_of,), jnp.float32, low / len(pieces), high / len(pieces)))
        level = level * jnp.repeat(draws, dims[dim] // shards_of).reshape([-1 if axis == dim else 1 for axis in range(len(dims))])
    return level


def setup_inputs(seed: int = 0) -> dict:
    seeds = jax.random.split(jax.random.key(seed), 6)
    return {
        "depth_start": jnp.clip(jax.random.uniform(seeds[0], (ROWS, COLS), jnp.float32, -0.3, 0.3) * block_levels(seeds[0], (ROWS, COLS), ((1, 128),), -0.4, 0.0), -0.3, 0.3),
        "albedo_start": jnp.clip(jnp.exp(math.log(2.0) - 1.3862944 * jax.random.uniform(seeds[1], (ROWS, COLS), jnp.float32) ** block_levels(seeds[1], (ROWS, COLS), ((1, 128),), -0.2, 0.2)), 0.5, 2.0),
        "observations": draw_observations(jax.random.fold_in(seeds[5], 71), 0),
        "light_table": plant(jax.random.randint(seeds[3], (NL, 4), 0, 1000), jax.random.fold_in(seeds[3], 1), 0, 999).astype(jnp.int32),
        "valid_mask": plant((jax.random.randint(seeds[4], (ROWS, COLS), 0, 8) < 7).astype(jnp.int32), jax.random.fold_in(seeds[4], 1), 0, 1),
    }


temper = 0.5
step_depth = 0.1
step_albedo = 0.2
epsilon = 1e-06

def decode_lights(table):
    values = table.astype(jnp.float32)
    light_x = (values[:, 0] / 500.0 - 1.0)[:, None, None]
    light_y = (values[:, 1] / 500.0 - 1.0)[:, None, None]
    light_z = (1.0 + values[:, 2] / 1000.0)[:, None, None]
    intensity = (0.5 + values[:, 3] / 1000.0)[:, None, None]
    return (light_x, light_y, light_z, intensity)

def shade_terms(surface, col_pad, row_pad, albedo, observed, table, valid, coord_x, coord_y):
    slope_x = 0.5 * (col_pad[:, 2:] - col_pad[:, :-2])
    slope_y = 0.5 * (row_pad[2:] - row_pad[:-2])
    light_x, light_y, light_z, intensity = decode_lights(table)
    delta_x = light_x - coord_x
    delta_y = light_y - coord_y
    delta_z = light_z - surface
    distance_sq = delta_x * delta_x + delta_y * delta_y + delta_z * delta_z
    norm_sq = 1.0 + slope_x * slope_x + slope_y * slope_y
    facing = -slope_x * delta_x - slope_y * delta_y + delta_z
    falloff = intensity / (distance_sq * jnp.sqrt(distance_sq) * jnp.sqrt(norm_sq))
    radiance = albedo * falloff * facing
    residual = valid * (radiance - observed.astype(jnp.float32))
    scores = -temper * residual * residual
    return (scores, residual, falloff, facing, delta_x, delta_y, delta_z, distance_sq, norm_sq, slope_x, slope_y)

def light_gradients(weights, terms, albedo):
    scores, residual, falloff, facing, delta_x, delta_y, delta_z, distance_sq, norm_sq, slope_x, slope_y = terms
    lit = weights * residual * falloff
    grad_albedo = lax.optimization_barrier(jnp.sum(lit * facing, axis=0))
    scaled = lit * albedo
    grad_direct = lax.optimization_barrier(jnp.sum(scaled * (-1.0 + 3.0 * facing * delta_z / distance_sq), axis=0))
    grad_x = lax.optimization_barrier(jnp.sum(scaled * (-delta_x - facing * slope_x / norm_sq), axis=0))
    grad_y = lax.optimization_barrier(jnp.sum(scaled * (-delta_y - facing * slope_y / norm_sq), axis=0))
    return (grad_x, grad_y, grad_direct, grad_albedo)

def depth_stencil(grad_x_pad, grad_y_pad, grad_direct):
    return grad_direct + 0.5 * (grad_x_pad[:, :-2] - grad_x_pad[:, 2:]) + 0.5 * (grad_y_pad[:-2] - grad_y_pad[2:])

def reference(depth_start, albedo_start, observations, light_table, valid_mask):
    surface = depth_start
    albedo = albedo_start
    valid = valid_mask.astype(jnp.float32)
    nrows, ncols = surface.shape
    coord_x = ((jnp.arange(ncols).astype(jnp.float32) + 0.5) / ncols - 0.5)[None, :]
    coord_y = ((jnp.arange(nrows).astype(jnp.float32) + 0.5 - nrows / 2.0) / ncols)[:, None]
    for iteration in range(ITERS):
        col_pad = jnp.pad(surface, ((0, 0), (1, 1)))
        row_pad = jnp.pad(surface, ((1, 1), (0, 0)))

        def first_pass(running, inputs):
            observed, table_row = inputs
            terms = shade_terms(surface, col_pad, row_pad, albedo, observed[None], table_row[None], valid, coord_x, coord_y)
            scores = terms[0][0]
            highest = jnp.maximum(running[0], scores)
            summed = running[1] * jnp.exp(running[0] - highest) + jnp.exp(scores - highest)
            return ((highest, summed), None)
        start_pair = (jnp.full(surface.shape, -jnp.inf, jnp.float32), jnp.zeros(surface.shape, jnp.float32))
        (highest, summed), unused = lax.scan(first_pass, start_pair, (observations, light_table))

        def second_pass(running, inputs):
            observed, table_row = inputs
            terms = shade_terms(surface, col_pad, row_pad, albedo, observed[None], table_row[None], valid, coord_x, coord_y)
            weights = jnp.exp(terms[0] - highest) / summed
            fields = light_gradients(weights, terms, albedo)
            return (tuple((running[index] + fields[index] for index in range(4))), None)
        zeros_four = tuple((jnp.zeros(surface.shape, jnp.float32) for index in range(4)))
        (grad_x, grad_y, grad_direct, grad_albedo), unused = lax.scan(second_pass, zeros_four, (observations, light_table))
        full_depth = depth_stencil(jnp.pad(grad_x, ((0, 0), (1, 1))), jnp.pad(grad_y, ((1, 1), (0, 0))), grad_direct)
        mean_depth = jnp.sum(full_depth * full_depth) / full_depth.size
        mean_albedo = jnp.sum(grad_albedo * grad_albedo) / grad_albedo.size
        surface = surface - step_depth * jnp.tanh(full_depth / jnp.sqrt(mean_depth + epsilon))
        albedo = albedo - step_albedo * jnp.tanh(grad_albedo / jnp.sqrt(mean_albedo + epsilon))
    return (surface, albedo)
```

```python
import functools
import math

import jax
import jax.numpy as jnp
from jax import lax
from jax.experimental import pallas as pl
from jax.experimental.pallas import tpu as pltpu
from jax.sharding import PartitionSpec as P

MESH = pl.DeviceIdType.MESH
ITERS = 2
step_depth = 0.1
step_albedo = 0.2
epsilon = 1e-06
LOG2E = 1.4426950408889634

UNIT_ROWS = 16
LANES = 128
f32 = jnp.float32


def remote(src, dst, send, recv, device):
    return pltpu.make_async_remote_copy(
        src_ref=src, dst_ref=dst, send_sem=send, recv_sem=recv, device_id=device, device_id_type=MESH
    )


def kernel(
    cfg,
    depth_hbm, albedo_hbm, obs_hbm, table_hbm, mask_hbm,
    depth_out, albedo_out,
    depth, albedo, mask, table, obs_all, tables, lights,
    dx2, c2, spad, gxpad, gypad, gd, pix,
    tt, ff, fp, gg,
    fd_all, ga_all, fd_side, sums,
    in_sem, ob_send, ob_recv, tb_send, tb_recv, sd_send, sd_recv,
    gx_send, gx_recv, gy_send, gy_recv, fs_send, fs_recv, fd_send, fd_recv, ar_send, ar_recv,
):
    NQ, NS, RQ, COLS, TOTAL, FACT = cfg
    nl = obs_hbm.shape[0]
    rows = depth_hbm.shape[0]
    ct = COLS // LANES
    nu = (RQ // UNIT_ROWS) * ct
    NL = NQ * nl
    q = lax.axis_index("light")
    s = lax.axis_index("strip")
    nz, ny, nx = FACT
    z, y, xh = s // (ny * nx), lax.rem(s, ny * nx) // nx, lax.rem(s, nx)
    mates = [(lax.rem(q + k, NQ), s) for k in (2, 3, 1)]
    right = (q, lax.rem(s + 1, NS))
    left = (q, lax.rem(s + NS - 1, NS))

    phases = [
        [(q, lax.rem(s + ny * nx * k, NS)) for k in range(1, nz)],
        [(q, z * (ny * nx) + lax.rem(y * nx + xh + nx * k, ny * nx)) for k in range(1, ny)],
        [
            (lax.rem(q + k, NQ), z * (ny * nx) + y * nx + lax.rem(xh + h, nx))
            for h in range(nx)
            for k in range(NQ)
            if (h, k) != (0, 0)
        ],
    ]
    slot = [z, y, q * nx + xh]
    counts = [nz, ny, NQ * nx]

    base = pl.multiple_of(q * RQ, RQ)
    ins = [
        pltpu.make_async_copy(depth_hbm, depth, in_sem.at[0]),
        pltpu.make_async_copy(albedo_hbm, albedo, in_sem.at[1]),
        pltpu.make_async_copy(mask_hbm, mask, in_sem.at[2]),
        pltpu.make_async_copy(table_hbm, table, in_sem.at[3]),
        pltpu.make_async_copy(
            obs_hbm.at[:, pl.ds(base, RQ), :], obs_all.at[pl.ds(q * nl, nl)], in_sem.at[4]
        ),
    ]
    for c in ins:
        c.start()

    barrier = pltpu.get_barrier_semaphore()
    partners = mates + [left, right] + [p for ph in phases for p in ph]
    for p in partners:
        pl.semaphore_signal(barrier, inc=1, device_id=p, device_id_type=MESH)
    pl.semaphore_wait(barrier, len(partners))

    ins[3].wait()
    tables[pl.ds(q, 1)] = jnp.zeros((1, nl, LANES), f32)
    tables[pl.ds(q, 1), :, 0:4] = table[...].astype(f32)[None]
    tb = []
    for j, p in enumerate(mates):
        c = remote(tables.at[q], tables.at[q], tb_send.at[j], tb_recv.at[j], p)
        c.start()
        tb.append(c)
    sd = [
        remote(
            depth_hbm.at[pl.ds(base, RQ), pl.ds(COLS - LANES, LANES)],
            spad.at[pl.ds(8, RQ), pl.ds(0, LANES)], sd_send.at[0], sd_recv.at[0], right,
        ),
        remote(
            depth_hbm.at[pl.ds(base, RQ), pl.ds(0, LANES)],
            spad.at[pl.ds(8, RQ), pl.ds(LANES + COLS, LANES)], sd_send.at[1], sd_recv.at[1], left,
        ),
    ]
    for c in sd:
        c.start()

    def unit_at(u):
        half, i = u // (nu // 2), lax.rem(u, nu // 2)
        row, k = i // (ct // 2), lax.rem(i, ct // 2)
        if ct == 4:
            col = k * (3 - 2 * half) + half
        else:
            col = half * (ct // 2) + k
        return pl.multiple_of(row * UNIT_ROWS, UNIT_ROWS), pl.multiple_of(col * LANES, LANES)

    def ob_copy(j, u):
        p = mates[j]
        r, c = unit_at(u)
        return remote(
            obs_hbm.at[:, pl.ds(pl.multiple_of(p[0] * RQ + r, UNIT_ROWS), UNIT_ROWS), pl.ds(c, LANES)],
            obs_all.at[pl.ds(q * nl, nl), pl.ds(r, UNIT_ROWS), pl.ds(c, LANES)],
            ob_send.at[j, u], ob_recv.at[j, u], p,
        )

    def send_obs(u, carry):
        for j in range(NQ - 1):
            ob_copy(j, u).start()
        return carry

    lax.fori_loop(0, nu, send_obs, 0)

    for c in tb:
        c.wait()
    tab = tables[...].reshape(NL, LANES)
    lx = tab[:, 0:1] / 500.0 - 1.0
    ly = tab[:, 1:2] / 500.0 - 1.0
    lz = 1.0 + tab[:, 2:3] / 1000.0
    le = 0.5 + tab[:, 3:4] / 1000.0
    for k, v in enumerate((lx, ly, lz, le)):
        lights[k] = jnp.broadcast_to(v, (NL, LANES))
    col_i = lax.broadcasted_iota(jnp.int32, (1, COLS), 1) + s * COLS
    px = (col_i.astype(f32) + 0.5) / TOTAL - 0.5
    row_i = lax.broadcasted_iota(jnp.int32, (RQ, 1), 0) + q * RQ
    py = (row_i.astype(f32) + 0.5 - rows / 2.0) / TOTAL
    d = lx - px
    for j in range(ct):
        v = d[:, j * LANES : (j + 1) * LANES]
        dx2[j] = v * v
    pyb = jnp.broadcast_to(py, (RQ, LANES))

    def make_c2(l, carry):
        dy = lights[1, pl.ds(l, 1), :] - pyb
        dy2 = dy * dy
        for j in range(ct):
            sl = pl.ds(j * LANES, LANES)
            c2[l, :, sl] = dy2 + dx2[j, pl.ds(l, 1), :]
        return carry

    lax.fori_loop(0, NL, make_c2, 0)

    for k in (0, 1, 2, 4):
        ins[k].wait()
    for c in sd:
        c.wait()

    top_r = pl.multiple_of(jnp.maximum(q * RQ - 8, 0), 8)
    bot_r = pl.multiple_of(jnp.minimum(q * RQ + RQ, rows - 8), 8)
    not_top = jnp.where(q == 0, 0.0, 1.0).astype(f32)
    not_bot = jnp.where(q == NQ - 1, 0.0, 1.0).astype(f32)
    not_left = jnp.where(s == 0, 0.0, 1.0).astype(f32)
    not_right = jnp.where(s == NS - 1, 0.0, 1.0).astype(f32)
    own = pl.ds(base, RQ)
    lt, mid, rt = pl.ds(0, LANES), pl.ds(LANES, COLS), pl.ds(LANES + COLS, LANES)

    def fill_surface(cur):
        spad[pl.ds(0, 8), mid] = cur[pl.ds(top_r, 8), :] * not_top
        spad[pl.ds(8, RQ), mid] = cur[own, :]
        spad[pl.ds(8 + RQ, 8), mid] = cur[pl.ds(bot_r, 8), :] * not_bot

    fill_surface(depth)
    spad[pl.ds(8, RQ), lt] = spad[pl.ds(8, RQ), lt] * not_left
    spad[pl.ds(8, RQ), rt] = spad[pl.ds(8, RQ), rt] * not_right

    width = COLS + 2 * LANES

    def shifted(ref):
        x = ref[...] if ref.shape[0] == RQ else ref[pl.ds(8, RQ), :]
        lo = pltpu.roll(x, 1, 1)[:, LANES : LANES + COLS]
        hi = pltpu.roll(x, width - 1, 1)[:, LANES : LANES + COLS]
        return lo, hi

    for it in range(ITERS):
        lo, hi = shifted(spad)
        sx = 0.5 * (hi - lo)
        sy = 0.5 * (spad[pl.ds(9, RQ), mid] - spad[pl.ds(7, RQ), mid])
        surf = spad[pl.ds(8, RQ), mid]
        nsq = 1.0 + sx * sx + sy * sy
        rn = lax.rsqrt(nsq)
        pix[0] = surf
        pix[1] = -surf + sx * px + sy * py
        pix[2] = sx
        pix[3] = sy
        pix[4] = albedo[own, :] * rn
        pix[5] = mask[own, :].astype(f32) * rn
        pix[6] = rn * rn
        pix[7] = jnp.broadcast_to(px, (RQ, COLS))

        def unit(u, carry):
            r, c = unit_at(u)
            rs, cs = pl.ds(r, UNIT_ROWS), pl.ds(c, LANES)
            if it == 0:
                for j in range(NQ - 1):
                    ob_copy(j, u).wait_recv()
            sv, qv, sxv, syv, av = (pix[k, rs, cs] for k in range(5))
            low = None
            for l in range(NL):
                ls = pl.ds(l, 1)
                lxv, lyv, lzv, lev = (lights[k, ls, :] for k in range(4))
                dz = lzv - sv
                dist = dz * dz + c2[l, rs, cs]
                facing = (qv + lzv) - sxv * lxv - syv * lyv
                ri = lax.rsqrt(dist)
                r2 = ri * ri
                fall = lev * (r2 * ri)
                fac = fall * facing
                t = av * fac - obs_all[l, rs, cs].astype(f32)
                tt[l] = t
                ff[l] = fall
                fp[l] = fac
                gg[l] = dz * r2
                uu = t * t
                low = uu if low is None else jnp.minimum(low, uu)
            low = low * (0.5 * LOG2E)
            acc = None
            for l in range(NL):
                ls = pl.ds(l, 1)
                t = tt[l]
                p = jnp.exp2(low - (0.5 * LOG2E) * (t * t))
                w = p * t
                pull = w * ff[l]
                pf = w * fp[l]
                new = (p, pf, pf * gg[l], pull, pull * lights[0, ls, :], pull * lights[1, ls, :])
                acc = new if acc is None else tuple(a + b for a, b in zip(acc, new))
            ssum, A, D, PU, X, Y = acc
            pyv = pyb[0:UNIT_ROWS] + r.astype(f32) / TOTAL
            pxv = pix[7, rs, cs]
            scale = pix[5, rs, cs] / ssum
            alb = albedo[pl.ds(pl.multiple_of(base + r, UNIT_ROWS), UNIT_ROWS), cs]
            inv_n = pix[6, rs, cs]
            ga = scale * A
            ca = scale * alb
            tilt = ga * alb * inv_n
            ga_all[it, pl.ds(pl.multiple_of(base + r, UNIT_ROWS), UNIT_ROWS), cs] = ga
            gd[rs, cs] = ca * (3.0 * D - PU)
            gxpad[it, rs, pl.ds(pl.multiple_of(c + LANES, LANES), LANES)] = (
                ca * (pxv * PU - X) - tilt * sxv
            )
            gypad[it, pl.ds(pl.multiple_of(r + 8, 8), UNIT_ROWS), cs] = ca * (pyv * PU - Y) - tilt * syv
            return carry

        lax.fori_loop(0, nu // 2, unit, 0)
        gx = [
            remote(
                gxpad.at[it, :, pl.ds(COLS, LANES)], gxpad.at[it, :, lt],
                gx_send.at[it, 0], gx_recv.at[it, 0], right,
            ),
            remote(
                gxpad.at[it, :, pl.ds(LANES, LANES)], gxpad.at[it, :, rt],
                gx_send.at[it, 1], gx_recv.at[it, 1], left,
            ),
        ]
        for c in gx:
            c.start()
        lax.fori_loop(nu // 2, nu, unit, 0)
        gy = [
            remote(
                gypad.at[it, pl.ds(RQ, 8)], gypad.at[it, pl.ds(0, 8)],
                gy_send.at[it, 0], gy_recv.at[it, 0], (lax.rem(q + 1, NQ), s),
            ),
            remote(
                gypad.at[it, pl.ds(8, 8)], gypad.at[it, pl.ds(RQ + 8, 8)],
                gy_send.at[it, 1], gy_recv.at[it, 1], (lax.rem(q + NQ - 1, NQ), s),
            ),
        ]
        for c in gy:
            c.start()
        for c in gx + gy:
            c.wait()
        gxpad[it, :, lt] = gxpad[it, :, lt] * not_left
        gxpad[it, :, rt] = gxpad[it, :, rt] * not_right
        gypad[it, pl.ds(0, 8)] = gypad[it, pl.ds(0, 8)] * not_top
        gypad[it, pl.ds(RQ + 8, 8)] = gypad[it, pl.ds(RQ + 8, 8)] * not_bot
        lo, hi = shifted(gxpad.at[it])
        fd = gd[...] + 0.5 * (lo - hi) + 0.5 * (gypad[it, pl.ds(7, RQ)] - gypad[it, pl.ds(9, RQ)])
        fd_all[it, own, :] = fd
        ga = ga_all[it, own, :]

        def lanes(v):
            v = jnp.sum(v, axis=0, keepdims=True)
            return functools.reduce(lambda a, b: a + b, [v[:, k * LANES : (k + 1) * LANES] for k in range(ct)])

        total = jnp.concatenate([lanes(fd * fd), lanes(ga * ga)], axis=0)
        fs, fg = [], []
        for k in range(3):
            sums[it, k, pl.ds(slot[k], 1)] = total[None]
            cs = []
            for p in phases[k]:
                c = remote(
                    sums.at[it, k, slot[k]], sums.at[it, k, slot[k]], ar_send.at[it, k], ar_recv.at[it, k], p
                )
                c.start()
            if k == 0:
                if it == 0:
                    fs = [
                        remote(
                            fd_all.at[it, own, pl.ds(COLS - LANES, LANES)], fd_side.at[0],
                            fs_send.at[0], fs_recv.at[0], right,
                        ),
                        remote(
                            fd_all.at[it, own, pl.ds(0, LANES)], fd_side.at[1],
                            fs_send.at[1], fs_recv.at[1], left,
                        ),
                    ]
                for j, p in enumerate(mates):
                    for m, ref in enumerate((fd_all, ga_all)):
                        fg.append(
                            remote(
                                ref.at[it, own], ref.at[it, own], fd_send.at[it, j, m], fd_recv.at[it, j, m], p
                            )
                        )
                for c in fs + fg:
                    c.start()
            n = counts[k] - 1
            if n:
                whole = sums.at[it, k, pl.ds(0, n)]
                w = remote(whole, whole, ar_send.at[it, k], ar_recv.at[it, k], phases[k][0])
                w.wait_recv()
                w.wait_send()
            total = jnp.sum(sums[it, k], axis=0)
        for c in fs + fg:
            c.wait()
        means = jnp.sum(total, axis=1, keepdims=True) / (rows * float(TOTAL))
        inv = 1.0 / jnp.sqrt(means + epsilon)
        inv_d, inv_a = inv[0:1, 0:1], inv[1:2, 0:1]
        last = it == ITERS - 1
        new_depth = depth[...] - step_depth * jnp.tanh(fd_all[it] * inv_d)
        new_albedo = albedo[...] - step_albedo * jnp.tanh(ga_all[it] * inv_a)
        if last:
            depth_out[...] = new_depth
            albedo_out[...] = new_albedo
        else:
            depth[...] = new_depth
            albedo[...] = new_albedo
            fill_surface(depth)
            for m, (side, keep) in enumerate(((lt, not_left), (rt, not_right))):
                v = spad[pl.ds(8, RQ), side]
                spad[pl.ds(8, RQ), side] = keep * (v - step_depth * jnp.tanh(fd_side[m] * inv_d))

    def drain(u, carry):
        for j in range(NQ - 1):
            ob_copy(j, u).wait_send()
        return carry

    lax.fori_loop(0, nu, drain, 0)


def factors(n):
    return {128: (8, 8, 2)}.get(n, (n // 2, 1, 2) if n % 2 == 0 else (n, 1, 1))


def solution(mesh):
    NQ, NS = mesh.shape["light"], mesh.shape["strip"]

    def shards(depth, albedo, obs, table, mask):
        rows, cols = depth.shape
        nl = obs.shape[0]
        RQ = rows // NQ
        FACT = factors(NS)
        NL = NQ * nl
        nu = (RQ // UNIT_ROWS) * (cols // LANES)
        cfg = (NQ, NS, RQ, cols, cols * NS, FACT)
        wide = cols + 2 * LANES
        V, D = pltpu.VMEM, pltpu.SemaphoreType.DMA
        any_spec = pl.BlockSpec(memory_space=pl.ANY)
        vm = pl.BlockSpec(memory_space=pltpu.VMEM)
        out = jax.ShapeDtypeStruct((rows, cols), f32)
        return pl.pallas_call(
            functools.partial(kernel, cfg),
            out_shape=(out, out),
            in_specs=[any_spec] * 5,
            out_specs=(vm, vm),
            scratch_shapes=[
                V((rows, cols), f32), V((rows, cols), f32), V((rows, cols), jnp.int32), V((nl, 4), jnp.int32),
                V((NL, RQ, cols), jnp.bfloat16), V((NQ, nl, LANES), f32), V((4, NL, LANES), f32),
                V((cols // LANES, NL, LANES), f32), V((NL, RQ, cols), f32),
                V((RQ + 16, wide), f32), V((ITERS, RQ, wide), f32), V((ITERS, RQ + 16, cols), f32),
                V((RQ, cols), f32), V((8, RQ, cols), f32),
                V((NL, UNIT_ROWS, LANES), f32), V((NL, UNIT_ROWS, LANES), f32),
                V((NL, UNIT_ROWS, LANES), f32), V((NL, UNIT_ROWS, LANES), f32),
                V((ITERS, rows, cols), f32), V((ITERS, rows, cols), f32),
                V((2, RQ, LANES), f32), V((ITERS, 3, 8, 2, LANES), f32),
                D((5,)), D((NQ - 1, nu)), D((NQ - 1, nu)), D((NQ - 1,)), D((NQ - 1,)), D((2,)), D((2,)),
                D((ITERS, 2)), D((ITERS, 2)), D((ITERS, 2)), D((ITERS, 2)), D((2,)), D((2,)),
                D((ITERS, NQ - 1, 2)), D((ITERS, NQ - 1, 2)), D((ITERS, 3)), D((ITERS, 3)),
            ],
            compiler_params=pltpu.CompilerParams(
                collective_id=0, has_side_effects=True, vmem_limit_bytes=28 * 2**20
            ),
            cost_estimate=pl.CostEstimate(flops=10**8, bytes_accessed=3 * 2**20, transcendentals=10**6),
            name="steps",
        )(depth, albedo, obs, table, mask)

    in_specs = (
        P(None, "strip"),
        P(None, "strip"),
        P("light", None, "strip"),
        P("light", None),
        P(None, "strip"),
    )
    return jax.shard_map(
        shards, mesh=mesh, in_specs=in_specs, out_specs=(P(None, "strip"), P(None, "strip")), check_vma=False
    )
```

```python
import functools
import math

import jax
import jax.numpy as jnp
from jax import lax
from jax.experimental import pallas as pl
from jax.experimental.pallas import tpu as pltpu
from jax.sharding import PartitionSpec as P

MESH = pl.DeviceIdType.MESH
ITERS = 2
step_depth = 0.1
step_albedo = 0.2
epsilon = 1e-06
LOG2E = 1.4426950408889634

UNIT_ROWS = 16
LANES = 128
f32 = jnp.float32


def remote(src, dst, send, recv, device):
    return pltpu.make_async_remote_copy(
        src_ref=src, dst_ref=dst, send_sem=send, recv_sem=recv, device_id=device, device_id_type=MESH
    )


def kernel(
    cfg,
    depth_hbm, albedo_hbm, obs_hbm, table_hbm, mask_hbm,
    depth_out, albedo_out,
    depth, albedo, mask, table, obs_all, tables, lights,
    dx2, c2, spad, gxpad, gypad, gd, pix,
    tt, ff, fp, gg,
    fd_all, ga_all, fd_side, plane_sums, group_sums,
    in_sem, ob_send, ob_recv, tb_send, tb_recv, sd_send, sd_recv,
    gx_send, gx_recv, gy_send, gy_recv, fs_send, fs_recv, fd_send, fd_recv, ar_send, ar_recv,
):
    NQ, NS, RQ, COLS, TOTAL, FACT = cfg
    nl = obs_hbm.shape[0]
    rows = depth_hbm.shape[0]
    ct = COLS // LANES
    nu = (RQ // UNIT_ROWS) * ct
    NL = NQ * nl
    q = lax.axis_index("light")
    s = lax.axis_index("strip")
    nz, ny, nx = FACT
    z, y, xh = s // (ny * nx), lax.rem(s, ny * nx) // nx, lax.rem(s, nx)
    mates = [(lax.rem(q + k, NQ), s) for k in (2, 3, 1)]
    right = (q, lax.rem(s + 1, NS))
    left = (q, lax.rem(s + NS - 1, NS))

    def ring(k, n):
        return min(k, n - k)

    plane = sorted(
        [(a, b) for a in range(nz) for b in range(ny) if (a, b) != (0, 0)],
        key=lambda o: -(ring(o[0], nz) + ring(o[1], ny)),
    )
    phases = [
        [(q, lax.rem(z + a, nz) * (ny * nx) + lax.rem(y + b, ny) * nx + xh) for a, b in plane],
        [
            (lax.rem(q + k, NQ), z * (ny * nx) + y * nx + lax.rem(xh + h, nx))
            for h in reversed(range(nx))
            for k in (2, 3, 1, 0)
            if (h, k) != (0, 0)
        ],
    ]
    slot = [z * ny + y, q * nx + xh]
    counts = [nz * ny, NQ * nx]

    base = pl.multiple_of(q * RQ, RQ)
    ins = [
        pltpu.make_async_copy(depth_hbm, depth, in_sem.at[0]),
        pltpu.make_async_copy(albedo_hbm, albedo, in_sem.at[1]),
        pltpu.make_async_copy(mask_hbm, mask, in_sem.at[2]),
        pltpu.make_async_copy(table_hbm, table, in_sem.at[3]),
        pltpu.make_async_copy(
            obs_hbm.at[:, pl.ds(base, RQ), :], obs_all.at[pl.ds(q * nl, nl)], in_sem.at[4]
        ),
    ]
    for c in ins:
        c.start()

    barrier = pltpu.get_barrier_semaphore()
    partners = mates + [left, right] + [p for ph in phases for p in ph]
    for p in partners:
        pl.semaphore_signal(barrier, inc=1, device_id=p, device_id_type=MESH)
    pl.semaphore_wait(barrier, len(partners))

    ins[3].wait()
    tables[pl.ds(q, 1)] = jnp.zeros((1, 4, LANES), f32)
    tables[pl.ds(q, 1), :, 0:nl] = table[...].astype(f32)[None]
    tb = []
    for j, p in enumerate(mates):
        c = remote(tables.at[q], tables.at[q], tb_send.at[j], tb_recv.at[j], p)
        c.start()
        tb.append(c)
    sd = [
        remote(
            depth_hbm.at[pl.ds(base, RQ), pl.ds(COLS - LANES, LANES)],
            spad.at[pl.ds(8, RQ), pl.ds(0, LANES)], sd_send.at[0], sd_recv.at[0], right,
        ),
        remote(
            depth_hbm.at[pl.ds(base, RQ), pl.ds(0, LANES)],
            spad.at[pl.ds(8, RQ), pl.ds(LANES + COLS, LANES)], sd_send.at[1], sd_recv.at[1], left,
        ),
    ]
    for c in sd:
        c.start()

    def unit_at(u):
        half, i = u // (nu // 2), lax.rem(u, nu // 2)
        row, k = i // (ct // 2), lax.rem(i, ct // 2)
        if ct == 4:
            col = k * (3 - 2 * half) + half
        else:
            col = half * (ct // 2) + k
        return pl.multiple_of(row * UNIT_ROWS, UNIT_ROWS), pl.multiple_of(col * LANES, LANES)

    def ob_copy(j, u):
        p = mates[j]
        r, c = unit_at(u)
        return remote(
            obs_hbm.at[:, pl.ds(pl.multiple_of(p[0] * RQ + r, UNIT_ROWS), UNIT_ROWS), pl.ds(c, LANES)],
            obs_all.at[pl.ds(q * nl, nl), pl.ds(r, UNIT_ROWS), pl.ds(c, LANES)],
            ob_send.at[j, u], ob_recv.at[j, u], p,
        )

    def send_obs(u, carry):
        for j in range(NQ - 1):
            ob_copy(j, u).start()
        return carry

    lax.fori_loop(0, nu, send_obs, 0)

    for c in tb:
        c.wait()
    diagonal = lax.broadcasted_iota(jnp.int32, (nl, LANES), 0) == lax.broadcasted_iota(
        jnp.int32, (nl, LANES), 1
    )

    def component(k):
        return jnp.concatenate(
            [
                jnp.sum(jnp.where(diagonal, tables[g, k : k + 1, :], 0.0), axis=1, keepdims=True)
                for g in range(NQ)
            ],
            axis=0,
        )

    lx = component(0) / 500.0 - 1.0
    ly = component(1) / 500.0 - 1.0
    lz = 1.0 + component(2) / 1000.0
    le = 0.5 + component(3) / 1000.0
    for k, v in enumerate((lx, ly, lz, le)):
        lights[k] = jnp.broadcast_to(v, (NL, LANES))
    col_i = lax.broadcasted_iota(jnp.int32, (1, COLS), 1) + s * COLS
    px = (col_i.astype(f32) + 0.5) / TOTAL - 0.5
    row_i = lax.broadcasted_iota(jnp.int32, (RQ, 1), 0) + q * RQ
    py = (row_i.astype(f32) + 0.5 - rows / 2.0) / TOTAL
    d = lx - px
    for j in range(ct):
        v = d[:, j * LANES : (j + 1) * LANES]
        dx2[j] = v * v
    pyb = jnp.broadcast_to(py, (RQ, LANES))

    def make_c2(l, carry):
        dy = lights[1, pl.ds(l, 1), :] - pyb
        dy2 = dy * dy
        for j in range(ct):
            sl = pl.ds(j * LANES, LANES)
            c2[l, :, sl] = dy2 + dx2[j, pl.ds(l, 1), :]
        return carry

    lax.fori_loop(0, NL, make_c2, 0)

    for k in (0, 1, 2, 4):
        ins[k].wait()
    for c in sd:
        c.wait()

    top_r = pl.multiple_of(jnp.maximum(q * RQ - 8, 0), 8)
    bot_r = pl.multiple_of(jnp.minimum(q * RQ + RQ, rows - 8), 8)
    not_top = jnp.where(q == 0, 0.0, 1.0).astype(f32)
    not_bot = jnp.where(q == NQ - 1, 0.0, 1.0).astype(f32)
    not_left = jnp.where(s == 0, 0.0, 1.0).astype(f32)
    not_right = jnp.where(s == NS - 1, 0.0, 1.0).astype(f32)
    own = pl.ds(base, RQ)
    lt, mid, rt = pl.ds(0, LANES), pl.ds(LANES, COLS), pl.ds(LANES + COLS, LANES)

    def fill_surface(cur):
        spad[pl.ds(0, 8), mid] = cur[pl.ds(top_r, 8), :] * not_top
        spad[pl.ds(8, RQ), mid] = cur[own, :]
        spad[pl.ds(8 + RQ, 8), mid] = cur[pl.ds(bot_r, 8), :] * not_bot

    fill_surface(depth)
    spad[pl.ds(8, RQ), lt] = spad[pl.ds(8, RQ), lt] * not_left
    spad[pl.ds(8, RQ), rt] = spad[pl.ds(8, RQ), rt] * not_right

    width = COLS + 2 * LANES

    def shifted(ref):
        x = ref[...] if ref.shape[0] == RQ else ref[pl.ds(8, RQ), :]
        lo = pltpu.roll(x, 1, 1)[:, LANES : LANES + COLS]
        hi = pltpu.roll(x, width - 1, 1)[:, LANES : LANES + COLS]
        return lo, hi

    sent = []
    for it in range(ITERS):
        lo, hi = shifted(spad)
        sx = 0.5 * (hi - lo)
        sy = 0.5 * (spad[pl.ds(9, RQ), mid] - spad[pl.ds(7, RQ), mid])
        surf = spad[pl.ds(8, RQ), mid]
        nsq = 1.0 + sx * sx + sy * sy
        rn = lax.rsqrt(nsq)
        pix[0] = surf
        pix[1] = -surf + sx * px + sy * py
        pix[2] = sx
        pix[3] = sy
        pix[4] = albedo[own, :] * rn
        pix[5] = mask[own, :].astype(f32) * rn
        pix[6] = rn * rn
        pix[7] = jnp.broadcast_to(px, (RQ, COLS))

        def unit(u, carry):
            r, c = unit_at(u)
            rs, cs = pl.ds(r, UNIT_ROWS), pl.ds(c, LANES)
            if it == 0:
                for j in range(NQ - 1):
                    ob_copy(j, u).wait_recv()
            sv, qv, sxv, syv, av = (pix[k, rs, cs] for k in range(5))
            low = None
            for l in range(NL):
                ls = pl.ds(l, 1)
                lxv, lyv, lzv, lev = (lights[k, ls, :] for k in range(4))
                dz = lzv - sv
                dist = dz * dz + c2[l, rs, cs]
                facing = (qv + lzv) - sxv * lxv - syv * lyv
                ri = lax.rsqrt(dist)
                r2 = ri * ri
                fall = lev * (r2 * ri)
                fac = fall * facing
                t = av * fac - obs_all[l, rs, cs].astype(f32)
                tt[l] = t
                ff[l] = fall
                fp[l] = fac
                gg[l] = dz * r2
                uu = t * t
                low = uu if low is None else jnp.minimum(low, uu)
            low = low * (0.5 * LOG2E)
            acc = None
            for l in range(NL):
                ls = pl.ds(l, 1)
                t = tt[l]
                p = jnp.exp2(low - (0.5 * LOG2E) * (t * t))
                w = p * t
                pull = w * ff[l]
                pf = w * fp[l]
                new = (p, pf, pf * gg[l], pull, pull * lights[0, ls, :], pull * lights[1, ls, :])
                acc = new if acc is None else tuple(a + b for a, b in zip(acc, new))
            ssum, A, D, PU, X, Y = acc
            pyv = pyb[0:UNIT_ROWS] + r.astype(f32) / TOTAL
            pxv = pix[7, rs, cs]
            scale = pix[5, rs, cs] / ssum
            alb = albedo[pl.ds(pl.multiple_of(base + r, UNIT_ROWS), UNIT_ROWS), cs]
            inv_n = pix[6, rs, cs]
            ga = scale * A
            ca = scale * alb
            tilt = ga * alb * inv_n
            ga_all[it, pl.ds(pl.multiple_of(base + r, UNIT_ROWS), UNIT_ROWS), cs] = ga
            gd[rs, cs] = ca * (3.0 * D - PU)
            gxpad[it, rs, pl.ds(pl.multiple_of(c + LANES, LANES), LANES)] = (
                ca * (pxv * PU - X) - tilt * sxv
            )
            gypad[it, pl.ds(pl.multiple_of(r + 8, 8), UNIT_ROWS), cs] = ca * (pyv * PU - Y) - tilt * syv
            return carry

        lax.fori_loop(0, nu // 2, unit, 0)
        gx = [
            remote(
                gxpad.at[it, :, pl.ds(COLS, LANES)], gxpad.at[it, :, lt],
                gx_send.at[it, 0], gx_recv.at[it, 0], right,
            ),
            remote(
                gxpad.at[it, :, pl.ds(LANES, LANES)], gxpad.at[it, :, rt],
                gx_send.at[it, 1], gx_recv.at[it, 1], left,
            ),
        ]
        for c in gx:
            c.start()
        lax.fori_loop(nu // 2, nu, unit, 0)
        gy = [
            remote(
                gypad.at[it, pl.ds(RQ, 8)], gypad.at[it, pl.ds(0, 8)],
                gy_send.at[it, 0], gy_recv.at[it, 0], (lax.rem(q + 1, NQ), s),
            ),
            remote(
                gypad.at[it, pl.ds(8, 8)], gypad.at[it, pl.ds(RQ + 8, 8)],
                gy_send.at[it, 1], gy_recv.at[it, 1], (lax.rem(q + NQ - 1, NQ), s),
            ),
        ]
        for c in gy:
            c.start()
        for c in gx + gy:
            c.wait()
        gxpad[it, :, lt] = gxpad[it, :, lt] * not_left
        gxpad[it, :, rt] = gxpad[it, :, rt] * not_right
        gypad[it, pl.ds(0, 8)] = gypad[it, pl.ds(0, 8)] * not_top
        gypad[it, pl.ds(RQ + 8, 8)] = gypad[it, pl.ds(RQ + 8, 8)] * not_bot
        lo, hi = shifted(gxpad.at[it])
        fd = gd[...] + 0.5 * (lo - hi) + 0.5 * (gypad[it, pl.ds(7, RQ)] - gypad[it, pl.ds(9, RQ)])
        fd_all[it, own, :] = fd
        ga = ga_all[it, own, :]

        def lanes(v):
            v = jnp.sum(v, axis=0, keepdims=True)
            return functools.reduce(lambda a, b: a + b, [v[:, k * LANES : (k + 1) * LANES] for k in range(ct)])

        total = jnp.concatenate([lanes(fd * fd), lanes(ga * ga)], axis=0)
        fs, fg = [], []
        for k, sums in enumerate((plane_sums, group_sums)):
            sums[it, pl.ds(slot[k], 1)] = total[None]
            mine = sums.at[it, slot[k]]
            for p in phases[k]:
                remote(mine, mine, ar_send.at[it, k], ar_recv.at[it, k], p).start()
            if k == 0:
                if it == 0:
                    fs = [
                        remote(
                            fd_all.at[it, own, pl.ds(COLS - LANES, LANES)], fd_side.at[0],
                            fs_send.at[0], fs_recv.at[0], right,
                        ),
                        remote(
                            fd_all.at[it, own, pl.ds(0, LANES)], fd_side.at[1],
                            fs_send.at[1], fs_recv.at[1], left,
                        ),
                    ]
                for j, p in enumerate(mates):
                    for m, ref in enumerate((fd_all, ga_all)):
                        fg.append(
                            remote(
                                ref.at[it, own], ref.at[it, own], fd_send.at[it, j, m], fd_recv.at[it, j, m], p
                            )
                        )
                for c in fs + fg:
                    c.start()
            n = counts[k] - 1
            if n:
                whole = sums.at[it, pl.ds(0, n)]
                w = remote(whole, whole, ar_send.at[it, k], ar_recv.at[it, k], phases[k][0])
                w.wait_recv()
                sent.append(w)
            total = jnp.sum(sums[it], axis=0)
        for c in fs + fg:
            c.wait()
        means = jnp.sum(total, axis=1, keepdims=True) / (rows * float(TOTAL))
        inv = 1.0 / jnp.sqrt(means + epsilon)
        inv_d, inv_a = inv[0:1, 0:1], inv[1:2, 0:1]
        last = it == ITERS - 1
        new_depth = depth[...] - step_depth * jnp.tanh(fd_all[it] * inv_d)
        new_albedo = albedo[...] - step_albedo * jnp.tanh(ga_all[it] * inv_a)
        if last:
            depth_out[...] = new_depth
            albedo_out[...] = new_albedo
        else:
            depth[...] = new_depth
            albedo[...] = new_albedo
            fill_surface(depth)
            for m, (side, keep) in enumerate(((lt, not_left), (rt, not_right))):
                v = spad[pl.ds(8, RQ), side]
                spad[pl.ds(8, RQ), side] = keep * (v - step_depth * jnp.tanh(fd_side[m] * inv_d))

    def drain(u, carry):
        for j in range(NQ - 1):
            ob_copy(j, u).wait_send()
        return carry

    lax.fori_loop(0, nu, drain, 0)
    for w in sent:
        w.wait_send()


def factors(n):
    return {128: (8, 8, 2)}.get(n, (n // 2, 1, 2) if n % 2 == 0 else (n, 1, 1))


def solution(mesh):
    NQ, NS = mesh.shape["light"], mesh.shape["strip"]

    def shards(depth, albedo, obs, table, mask):
        rows, cols = depth.shape
        nl = obs.shape[0]
        RQ = rows // NQ
        FACT = factors(NS)
        NL = NQ * nl
        nu = (RQ // UNIT_ROWS) * (cols // LANES)
        cfg = (NQ, NS, RQ, cols, cols * NS, FACT)
        wide = cols + 2 * LANES
        V, D = pltpu.VMEM, pltpu.SemaphoreType.DMA
        any_spec = pl.BlockSpec(memory_space=pl.ANY)
        vm = pl.BlockSpec(memory_space=pltpu.VMEM)
        out = jax.ShapeDtypeStruct((rows, cols), f32)
        return pl.pallas_call(
            functools.partial(kernel, cfg),
            out_shape=(out, out),
            in_specs=[any_spec] * 5,
            out_specs=(vm, vm),
            scratch_shapes=[
                V((rows, cols), f32), V((rows, cols), f32), V((rows, cols), jnp.int32), V((4, nl), jnp.int32),
                V((NL, RQ, cols), jnp.bfloat16), V((NQ, 4, LANES), f32), V((4, NL, LANES), f32),
                V((cols // LANES, NL, LANES), f32), V((NL, RQ, cols), f32),
                V((RQ + 16, wide), f32), V((ITERS, RQ, wide), f32), V((ITERS, RQ + 16, cols), f32),
                V((RQ, cols), f32), V((8, RQ, cols), f32),
                V((NL, UNIT_ROWS, LANES), f32), V((NL, UNIT_ROWS, LANES), f32),
                V((NL, UNIT_ROWS, LANES), f32), V((NL, UNIT_ROWS, LANES), f32),
                V((ITERS, rows, cols), f32), V((ITERS, rows, cols), f32),
                V((2, RQ, LANES), f32),
                V((ITERS, FACT[0] * FACT[1], 2, LANES), f32), V((ITERS, NQ * FACT[2], 2, LANES), f32),
                D((5,)), D((NQ - 1, nu)), D((NQ - 1, nu)), D((NQ - 1,)), D((NQ - 1,)), D((2,)), D((2,)),
                D((ITERS, 2)), D((ITERS, 2)), D((ITERS, 2)), D((ITERS, 2)), D((2,)), D((2,)),
                D((ITERS, NQ - 1, 2)), D((ITERS, NQ - 1, 2)), D((ITERS, 2)), D((ITERS, 2)),
            ],
            compiler_params=pltpu.CompilerParams(
                collective_id=0, has_side_effects=True, vmem_limit_bytes=56 * 2**20
            ),
            cost_estimate=pl.CostEstimate(flops=10**8, bytes_accessed=3 * 2**20, transcendentals=10**6),
            name="steps",
        )(depth, albedo, obs, table.T, mask)

    in_specs = (
        P(None, "strip"),
        P(None, "strip"),
        P("light", None, "strip"),
        P("light", None),
        P(None, "strip"),
    )
    return jax.shard_map(
        shards, mesh=mesh, in_specs=in_specs, out_specs=(P(None, "strip"), P(None, "strip")), check_vma=False
    )
```

```python
import functools

import jax
import jax.numpy as jnp
from jax import lax
from jax.experimental import pallas as pl
from jax.experimental.pallas import tpu as pltpu
from jax.sharding import PartitionSpec as P

MESH = pl.DeviceIdType.MESH
ITERS = 2
step_depth = 0.1
step_albedo = 0.2
epsilon = 1e-06
HALF_LOG2E = 0.5 * 1.4426950408889634

UNIT = 16
LANES = 128
f32 = jnp.float32


def remote(src, dst, send, recv, device):
    return pltpu.make_async_remote_copy(
        src_ref=src, dst_ref=dst, send_sem=send, recv_sem=recv, device_id=device, device_id_type=MESH
    )


def kernel(
    cfg,
    depth_hbm, albedo_hbm, obs_hbm, table_hbm, mask_hbm,
    depth_out, albedo_out,
    depth, albedo, mask, table, obs_own, obs_all, tables, lights,
    staged, dx2, c2, spad, alb_own, gx, gypad, gd, pix,
    tt, ff, fp, gg,
    edge_obs, halo_obs, halo_loop, pack_out, pack_in, halo,
    fd_all, ga_all, near_sums, far_sums,
    in_sem, st_sem, ob_send, ob_recv, tb_send, tb_recv, eo_send, eo_recv, lo_send, lo_recv,
    pk_send, pk_recv, fd_send, fd_recv, ar_send, ar_recv,
):
    NQ, NS, COLS, TOTAL, FACT = cfg
    nl = obs_hbm.shape[0]
    rows = depth_hbm.shape[0]
    nu = rows // UNIT
    NL = NQ * nl
    q = lax.axis_index("light")
    s = lax.axis_index("strip")
    nz, ny, nx = FACT
    z, y, xh = s // (ny * nx), lax.rem(s, ny * nx) // nx, lax.rem(s, nx)
    up, down = lax.rem(s + 1, NS), lax.rem(s + NS - 1, NS)
    others = [lax.rem(q + k, NQ) for k in (2, 3, 1)]
    across, mate = (q ^ 2, s), (q ^ 1, s)
    right = (lax.rem(q + 1, NQ), jnp.where(q == NQ - 1, up, s))
    left = (lax.rem(q + NQ - 1, NQ), jnp.where(q == 0, down, s))

    def ring(k, n):
        return min(k, n - k)

    plane = sorted(
        [(a, b) for a in range(nz) for b in range(ny) if (a, b) != (0, 0)],
        key=lambda o: -(ring(o[0], nz) + ring(o[1], ny)),
    )
    phases = [
        [
            (lax.rem(q + k, NQ), z * (ny * nx) + y * nx + lax.rem(xh + h, nx))
            for h in reversed(range(nx))
            for k in (2, 3, 1, 0)
            if (h, k) != (0, 0)
        ],
        [(q, lax.rem(z + a, nz) * (ny * nx) + lax.rem(y + b, ny) * nx + xh) for a, b in plane],
    ]
    slot = [q * nx + xh, z * ny + y]
    counts = [NQ * nx, nz * ny]

    base = pl.multiple_of(q * LANES, LANES)
    own = pl.ds(base, LANES)
    ins = [
        pltpu.make_async_copy(table_hbm, table, in_sem.at[0]),
        pltpu.make_async_copy(depth_hbm, depth, in_sem.at[1]),
        pltpu.make_async_copy(albedo_hbm, albedo, in_sem.at[2]),
        pltpu.make_async_copy(mask_hbm, mask, in_sem.at[3]),
        pltpu.make_async_copy(obs_hbm, obs_own, in_sem.at[4]),
    ]
    mine = pl.ds(pl.multiple_of(q * nl, nl), nl)

    def block(t, u):
        r = pl.ds(pl.multiple_of(u * UNIT, UNIT), UNIT)
        return obs_hbm.at[:, r, pl.ds(pl.multiple_of(t * LANES, LANES), LANES)]

    def stage(u, carry):
        for j, t in enumerate(others):
            pltpu.make_async_copy(block(t, u), staged.at[j, u], st_sem.at[j]).start()
        return carry

    def stage_own(u, carry):
        pltpu.make_async_copy(block(q, u), obs_all.at[u, mine], st_sem.at[NQ - 1]).start()
        return carry

    ins[0].start()
    lax.fori_loop(0, nu, stage, 0)
    lax.fori_loop(0, nu, stage_own, 0)
    for c in ins[1:]:
        c.start()

    barrier = pltpu.get_barrier_semaphore()
    beside = [(lax.rem(q + k, NQ), t) for k in range(NQ) for t in (up, down)]
    partners = phases[0] + beside + phases[1]
    for p in partners:
        pl.semaphore_signal(barrier, inc=1, device_id=p, device_id_type=MESH)

    def ob_copy(j, u):
        t = others[j]
        return remote(
            staged.at[j, u], obs_all.at[u, mine], ob_send.at[j, u], ob_recv.at[j, u], (t, s)
        )

    def send_obs(u, carry):
        for j in range(NQ - 1):
            ob_copy(j, u).start()
        return carry

    eye = lax.broadcasted_iota(jnp.int32, (rows, LANES), 0) == lax.broadcasted_iota(jnp.int32, (rows, LANES), 1)
    lane = lax.broadcasted_iota(jnp.int32, (rows, LANES), 1)
    lane1 = lax.broadcasted_iota(jnp.int32, (1, LANES), 1)

    def to_lanes(v, c):
        return jnp.sum(jnp.where(eye, jnp.broadcast_to(v[:, c : c + 1], (rows, LANES)), 0.0), axis=0, keepdims=True)

    def to_rows(v):
        return jnp.sum(jnp.where(eye, jnp.broadcast_to(v, (rows, LANES)), 0.0), axis=1, keepdims=True)

    def pack_edges(it, fields):
        k = 0
        for v, far in fields:
            pack_out[it, 0, k : k + 1, :] = to_lanes(v, LANES - 1)
            pack_out[it, 1, k : k + 1, :] = to_lanes(v, 0)
            k += 1
            if far:
                pack_out[it, 0, k : k + 1, :] = to_lanes(v, LANES - 2)
                pack_out[it, 1, k : k + 1, :] = to_lanes(v, 1)
                k += 1

    def send_edges(it):
        out = [
            remote(pack_out.at[it, 0], pack_in.at[it, 0], pk_send.at[it, 0], pk_recv.at[it, 0], right),
            remote(pack_out.at[it, 1], pack_in.at[it, 1], pk_send.at[it, 1], pk_recv.at[it, 1], left),
        ]
        for c in out:
            c.start()
        return out

    for k in (1, 2, 3):
        ins[k].wait()
    center = pl.ds(8, rows)
    spad[...] = jnp.zeros_like(spad)
    gypad[...] = jnp.zeros_like(gypad)
    pack_out[...] = jnp.zeros_like(pack_out)
    spad[center, :] = depth[:, own]
    alb_own[...] = albedo[:, own]
    pack_edges(
        0, ((depth[:, own], True), (alb_own[...], False), (mask[:, own].astype(f32), False))
    )

    ins[0].wait()
    tables[pl.ds(q, 1)] = jnp.zeros((1, 4, LANES), f32)
    tables[pl.ds(q, 1), :, 0:nl] = table[...].astype(f32)[None]
    ins[4].wait()
    e_row = lax.broadcasted_iota(jnp.int32, (2 * NQ, COLS), 0)
    e_col = lax.broadcasted_iota(jnp.int32, (2 * NQ, COLS), 1)
    wanted = lax.rem((e_row // 2) * LANES + jnp.where(lax.rem(e_row, 2) == 0, COLS - 1, LANES), COLS)
    pick = jnp.where(e_col == wanted, 1.0, 0.0).astype(jnp.bfloat16)
    for l in range(nl):
        got = lax.dot_general(
            pick, obs_own[l], (((1,), (1,)), ((), ())), preferred_element_type=f32
        )
        for e in range(2 * NQ):
            edge_obs[e, l : l + 1, :] = got[e : e + 1]
    pl.semaphore_wait(barrier, len(partners))
    tb = [
        remote(tables.at[q], tables.at[q], tb_send.at[j], tb_recv.at[j], (t, s)) for j, t in enumerate(others)
    ]
    for c in tb:
        c.start()

    pk = send_edges(0)
    eo = []
    for j, t in enumerate(others):
        for side in range(2):
            strip = jnp.where(t == 0, up, s) if side == 0 else jnp.where(t == NQ - 1, down, s)
            eo.append(
                remote(
                    edge_obs.at[2 * t + side], halo_obs.at[side, mine],
                    eo_send.at[j, side], eo_recv.at[j, side], (t, strip),
                )
            )
    lo = [
        remote(edge_obs.at[0], halo_loop.at[0], lo_send.at[0], lo_recv.at[0], (q, up)),
        remote(edge_obs.at[2 * NQ - 1], halo_loop.at[1], lo_send.at[1], lo_recv.at[1], (q, down)),
    ]
    for c in eo + lo:
        c.start()

    for j in range(NQ - 1):
        pltpu.make_async_copy(staged.at[j], staged.at[j], st_sem.at[j]).wait()
    lax.fori_loop(0, nu, send_obs, 0)

    for c in tb:
        c.wait()
    diagonal = lax.broadcasted_iota(jnp.int32, (nl, LANES), 0) == lax.broadcasted_iota(jnp.int32, (nl, LANES), 1)

    def component(k):
        return jnp.concatenate(
            [
                jnp.sum(jnp.where(diagonal, tables[g, k : k + 1, :], 0.0), axis=1, keepdims=True)
                for g in range(NQ)
            ],
            axis=0,
        )

    lx = component(0) / 500.0 - 1.0
    ly = component(1) / 500.0 - 1.0
    lz = 1.0 + component(2) / 1000.0
    le = 0.5 + component(3) / 1000.0
    for k, v in enumerate((lx, ly, lz, le)):
        lights[k] = jnp.broadcast_to(v, (NL, LANES))

    def coord_x(columns):
        return (columns.astype(f32) + 0.5) / TOTAL - 0.5

    def coord_y(index):
        return (index.astype(f32) + 0.5 - rows / 2.0) / TOTAL

    first = s * COLS + q * LANES
    px = coord_x(lane1 + first)
    py = coord_y(lax.broadcasted_iota(jnp.int32, (rows, LANES), 0))
    py_lane = coord_y(lane1)
    d = lx - px
    dx2[...] = d * d

    def make_c2(l, carry):
        dy = lights[1, pl.ds(l, 1), :] - py
        c2[l] = dy * dy + dx2[pl.ds(l, 1), :]
        return carry

    lax.fori_loop(0, NL, make_c2, 0)

    not_left = jnp.where((s == 0) & (q == 0), 0.0, 1.0).astype(f32)
    not_right = jnp.where((s == NS - 1) & (q == NQ - 1), 0.0, 1.0).astype(f32)
    keep = (not_left, not_right)

    for c in pk + eo + lo:
        c.wait()
    for side in range(2):
        inner = edge_obs[2 * q + side]
        at_end = (q == 0) if side == 0 else (q == NQ - 1)
        halo_obs[side, mine, :] = jnp.where(at_end, halo_loop[side], inner)
        v = pack_in[0, side]
        halo[side, 0:2, :] = v[0:2] * keep[side]
        halo[side, 2:4, :] = v[2:4]
    pltpu.make_async_copy(obs_all.at[:, mine], obs_all.at[:, mine], st_sem.at[NQ - 1]).wait()

    def widen(v, lo_col, hi_col):
        lo_v = jnp.where(lane == 0, lo_col, pltpu.roll(v, 1, 1))
        hi_v = jnp.where(lane == LANES - 1, hi_col, pltpu.roll(v, LANES - 1, 1))
        return lo_v, hi_v

    def side_gradient(side):
        near, far, alb, val = (halo[side, k : k + 1, :] for k in range(4))
        surf = spad[center, :]
        inside = to_lanes(surf, 0 if side == 0 else LANES - 1)
        sx = 0.5 * (inside - far) if side == 0 else 0.5 * (far - inside)
        below = jnp.where(lane1 == LANES - 1, 0.0, pltpu.roll(near, LANES - 1, 1))
        above = jnp.where(lane1 == 0, 0.0, pltpu.roll(near, 1, 1))
        sy = 0.5 * (below - above)
        nsq = 1.0 + sx * sx + sy * sy
        rn = lax.rsqrt(nsq)
        pxs = coord_x(jnp.full((1, LANES), first, jnp.int32) + (-1 if side == 0 else LANES))
        lxs, lys, lzs, les = (lights[k] for k in range(4))
        dx, dy, dz = lxs - pxs, lys - py_lane, lzs - near
        dist = dx * dx + dy * dy + dz * dz
        facing = dz - sx * dx - sy * dy
        ri = lax.rsqrt(dist)
        fall = les * (ri * ri * ri)
        t = (alb * rn) * (fall * facing) - halo_obs[side]
        uu = t * t
        p = jnp.exp2(HALF_LOG2E * (jnp.min(uu, axis=0, keepdims=True) - uu))
        pull = p * t * fall
        total = jnp.sum(p, axis=0, keepdims=True)
        inner = jnp.sum(pull * dx, axis=0, keepdims=True) + (sx * rn * rn) * jnp.sum(
            pull * facing, axis=0, keepdims=True
        )
        return to_rows(-(keep[side] * val * rn * alb / total) * inner)

    sent, gathered = [], []
    for it in range(ITERS):
        last = it == ITERS - 1
        surf = spad[center, :]
        lo_v, hi_v = widen(surf, to_rows(halo[0, 0:1, :]), to_rows(halo[1, 0:1, :]))
        sx = 0.5 * (hi_v - lo_v)
        sy = 0.5 * (spad[pl.ds(9, rows), :] - spad[pl.ds(7, rows), :])
        nsq = 1.0 + sx * sx + sy * sy
        rn = lax.rsqrt(nsq)
        pix[0] = surf
        pix[1] = -surf + sx * px + sy * py
        pix[2] = sx
        pix[3] = sy
        pix[4] = alb_own[...] * rn
        pix[5] = mask[:, own].astype(f32) * rn
        pix[6] = rn * rn
        gx_lo, gx_hi = side_gradient(0), side_gradient(1)

        def unit(u, carry):
            rs = pl.ds(pl.multiple_of(u * UNIT, UNIT), UNIT)
            if it == 0:
                for j in range(NQ - 1):
                    ob_copy(j, u).wait_recv()
            sv, qv, sxv, syv, av = (pix[k, rs, :] for k in range(5))
            low = None
            for l in range(NL):
                ls = pl.ds(l, 1)
                lxv, lyv, lzv, lev = (lights[k, ls, :] for k in range(4))
                dz = lzv - sv
                dist = dz * dz + c2[l, rs, :]
                facing = (qv + lzv) - sxv * lxv - syv * lyv
                ri = lax.rsqrt(dist)
                r2 = ri * ri
                fall = lev * (r2 * ri)
                fac = fall * facing
                t = av * fac - obs_all[u, l].astype(f32)
                tt[l] = t
                ff[l] = fall
                fp[l] = fac
                gg[l] = dz * r2
                uu = t * t
                low = uu if low is None else jnp.minimum(low, uu)
            low = low * HALF_LOG2E
            acc = None
            for l in range(NL):
                ls = pl.ds(l, 1)
                t = tt[l]
                p = jnp.exp2(low - HALF_LOG2E * (t * t))
                w = p * t
                pull = w * ff[l]
                pf = w * fp[l]
                new = (p, pf, pf * gg[l], pull, pull * lights[0, ls, :], pull * lights[1, ls, :])
                acc = new if acc is None else tuple(a + b for a, b in zip(acc, new))
            ssum, A, D, PU, X, Y = acc
            pyv = py[0:UNIT] + lax.convert_element_type(u * UNIT, f32) / TOTAL
            scale = pix[5, rs, :] / ssum
            alb = alb_own[rs, :]
            ga = scale * A
            ca = scale * alb
            tilt = ga * alb * pix[6, rs, :]
            ga_all[it, rs, own] = ga
            gd[rs, :] = ca * (3.0 * D - PU)
            gx[rs, :] = ca * (px * PU - X) - tilt * sxv
            gypad[pl.ds(pl.multiple_of(u * UNIT + 8, 8), UNIT), :] = ca * (pyv * PU - Y) - tilt * syv
            return carry

        lax.fori_loop(0, nu, unit, 0)
        lo_v, hi_v = widen(gx[...], gx_lo, gx_hi)
        fd = gd[...] + 0.5 * (lo_v - hi_v) + 0.5 * (gypad[pl.ds(7, rows), :] - gypad[pl.ds(9, rows), :])
        ga = ga_all[it, :, own]
        total = jnp.concatenate(
            [jnp.sum(fd * fd, axis=0, keepdims=True), jnp.sum(ga * ga, axis=0, keepdims=True)], axis=0
        )
        for k, sums in enumerate((near_sums, far_sums)):
            sums[it, pl.ds(slot[k], 1)] = total[None]
            part = sums.at[it, slot[k]]
            for p in phases[k]:
                remote(part, part, ar_send.at[it, k], ar_recv.at[it, k], p).start()
            if k == 0:
                fd_all[it, :, own] = fd
                theirs = pl.ds(pl.multiple_of((q ^ 2) * LANES, LANES), LANES)

                def moves(n, cols, device):
                    return [
                        remote(
                            ref.at[it, :, cols], ref.at[it, :, cols], fd_send.at[it, n, m], fd_recv.at[it, n, m], device
                        )
                        for m, ref in enumerate((fd_all, ga_all))
                    ]

                over, to_mate, onward = moves(0, own, across), moves(1, own, mate), moves(2, theirs, mate)
                if not last:
                    pack_edges(1, ((fd, True), (ga, False)))
                    pk = send_edges(1)
                for c in over + to_mate:
                    c.start()
            else:
                for c in over:
                    c.wait()
                for c in onward:
                    c.start()
                if last:
                    for c in gathered:
                        c.wait()
                    depth[...] = depth[...] - step_depth * jnp.tanh(fd_all[0] * inv_d)
                    albedo[...] = albedo[...] - step_albedo * jnp.tanh(ga_all[0] * inv_a)
            whole = sums.at[it, pl.ds(0, counts[k] - 1)]
            w = remote(whole, whole, ar_send.at[it, k], ar_recv.at[it, k], phases[k][0])
            w.wait_recv()
            sent.append(w)
            total = jnp.sum(sums[it], axis=0)
        means = jnp.sum(total, axis=1, keepdims=True) / (rows * float(TOTAL))
        inv = 1.0 / jnp.sqrt(means + epsilon)
        inv_d, inv_a = inv[0:1, 0:1], inv[1:2, 0:1]
        if last:
            for c in to_mate + onward:
                c.wait()
            depth_out[...] = depth[...] - step_depth * jnp.tanh(fd_all[it] * inv_d)
            albedo_out[...] = albedo[...] - step_albedo * jnp.tanh(ga_all[it] * inv_a)
        else:
            gathered = to_mate + onward
            spad[center, :] = spad[center, :] - step_depth * jnp.tanh(fd_all[it, :, own] * inv_d)
            alb_own[...] = alb_own[...] - step_albedo * jnp.tanh(ga_all[it, :, own] * inv_a)
            for c in pk:
                c.wait()
            for side in range(2):
                v = pack_in[1, side]
                halo[side, 0:2, :] = keep[side] * (halo[side, 0:2, :] - step_depth * jnp.tanh(v[0:2] * inv_d))
                halo[side, 2:3, :] = halo[side, 2:3, :] - step_albedo * jnp.tanh(v[2:3] * inv_a)

    def drain(u, carry):
        for j in range(NQ - 1):
            ob_copy(j, u).wait_send()
        return carry

    lax.fori_loop(0, nu, drain, 0)
    for w in sent:
        w.wait_send()


def factors(n):
    return {128: (8, 8, 2)}[n]


def solution(mesh):
    NQ, NS = mesh.shape["light"], mesh.shape["strip"]

    def shards(depth, albedo, obs, table, mask):
        rows, cols = depth.shape
        nl = obs.shape[0]
        FACT = factors(NS)
        NL = NQ * nl
        nu = rows // UNIT
        cfg = (NQ, NS, cols, cols * NS, FACT)
        V, D = pltpu.VMEM, pltpu.SemaphoreType.DMA
        any_spec = pl.BlockSpec(memory_space=pl.ANY)
        vm = pl.BlockSpec(memory_space=pltpu.VMEM)
        out = jax.ShapeDtypeStruct((rows, cols), f32)
        return pl.pallas_call(
            functools.partial(kernel, cfg),
            out_shape=(out, out),
            in_specs=[any_spec] * 5,
            out_specs=(vm, vm),
            scratch_shapes=[
                V((rows, cols), f32), V((rows, cols), f32), V((rows, cols), jnp.int32), V((4, nl), jnp.int32),
                V((nl, rows, cols), jnp.bfloat16), V((nu, NL, UNIT, LANES), jnp.bfloat16),
                V((NQ, 4, LANES), f32), V((4, NL, LANES), f32),
                V((NQ - 1, nu, nl, UNIT, LANES), jnp.bfloat16),
                V((NL, LANES), f32), V((NL, rows, LANES), f32), V((rows + 16, LANES), f32), V((rows, LANES), f32),
                V((rows, LANES), f32), V((rows + 16, LANES), f32), V((rows, LANES), f32), V((7, rows, LANES), f32),
                V((NL, UNIT, LANES), f32), V((NL, UNIT, LANES), f32),
                V((NL, UNIT, LANES), f32), V((NL, UNIT, LANES), f32),
                V((2 * NQ, nl, LANES), f32), V((2, NL, LANES), f32), V((2, nl, LANES), f32),
                V((ITERS, 2, 8, LANES), f32), V((ITERS, 2, 8, LANES), f32), V((2, 8, LANES), f32),
                V((ITERS, rows, cols), f32), V((ITERS, rows, cols), f32),
                V((ITERS, NQ * FACT[2], 2, LANES), f32), V((ITERS, FACT[0] * FACT[1], 2, LANES), f32),
                D((5,)), D((NQ,)), D((NQ - 1, nu)), D((NQ - 1, nu)), D((NQ - 1,)), D((NQ - 1,)),
                D((NQ - 1, 2)), D((NQ - 1, 2)), D((2,)), D((2,)),
                D((ITERS, 2)), D((ITERS, 2)), D((ITERS, 3, 2)), D((ITERS, 3, 2)), D((ITERS, 2)), D((ITERS, 2)),
            ],
            compiler_params=pltpu.CompilerParams(
                collective_id=0, has_side_effects=True, vmem_limit_bytes=56 * 2**20
            ),
            cost_estimate=pl.CostEstimate(flops=10**8, bytes_accessed=3 * 2**20, transcendentals=10**6),
            name="steps",
        )(depth, albedo, obs, table.T, mask)

    in_specs = (
        P(None, "strip"),
        P(None, "strip"),
        P("light", None, "strip"),
        P("light", None),
        P(None, "strip"),
    )
    return jax.shard_map(
        shards, mesh=mesh, in_specs=in_specs, out_specs=(P(None, "strip"), P(None, "strip")), check_vma=False
    )
```

```python
import functools

import jax
import jax.numpy as jnp
from jax import lax
from jax.experimental import pallas as pl
from jax.experimental.pallas import tpu as pltpu
from jax.sharding import PartitionSpec as P

MESH = pl.DeviceIdType.MESH
ITERS = 2
step_depth = 0.1
step_albedo = 0.2
epsilon = 1e-06
HALF_LOG2E = 0.5 * 1.4426950408889634
ROOT = HALF_LOG2E ** 0.5

UNIT = 16
AHEAD = 3
LANES = 128
f32 = jnp.float32


def remote(src, dst, send, recv, device):
    return pltpu.make_async_remote_copy(
        src_ref=src, dst_ref=dst, send_sem=send, recv_sem=recv, device_id=device, device_id_type=MESH
    )


def kernel(
    cfg,
    depth_hbm, albedo_hbm, obs_hbm, table_ref, mask_hbm,
    depth_out, albedo_out,
    depth, albedo, mask, obs_own, obs_all, tables, lights,
    staged, dx1, dy1, obs_f, c2, spad, alb_own, gx, gypad, gd, pix,
    tt, ff, fp, gg,
    edge_obs, halo_obs, halo_loop, pack_out, pack_in, halo,
    fd_all, ga_all, near_sums, far_sums,
    in_sem, st_sem, ob_send, ob_recv, tb_send, tb_recv, eo_send, eo_recv, lo_send, lo_recv,
    pk_send, pk_recv, fd_send, fd_recv, ar_send, ar_recv,
):
    NQ, NS, COLS, TOTAL, FACT = cfg
    nl = obs_hbm.shape[0]
    rows = depth_hbm.shape[0]
    nu = rows // UNIT
    NL = NQ * nl
    q = lax.axis_index("light")
    s = lax.axis_index("strip")
    nz, ny, nx = FACT
    z, y, xh = s // (ny * nx), lax.rem(s, ny * nx) // nx, lax.rem(s, nx)
    up, down = lax.rem(s + 1, NS), lax.rem(s + NS - 1, NS)
    others = [lax.rem(q + k, NQ) for k in (2, 3, 1)]
    across, mate = (q ^ 2, s), (q ^ 1, s)
    right = (lax.rem(q + 1, NQ), jnp.where(q == NQ - 1, up, s))
    left = (lax.rem(q + NQ - 1, NQ), jnp.where(q == 0, down, s))

    def ring(k, n):
        return min(k, n - k)

    plane = sorted(
        [(a, b) for a in range(nz) for b in range(ny) if (a, b) != (0, 0)],
        key=lambda o: -(ring(o[0], nz) + ring(o[1], ny)),
    )
    phases = [
        [
            (lax.rem(q + k, NQ), z * (ny * nx) + y * nx + lax.rem(xh + h, nx))
            for h in reversed(range(nx))
            for k in (2, 3, 1, 0)
            if (h, k) != (0, 0)
        ],
        [(q, lax.rem(z + a, nz) * (ny * nx) + lax.rem(y + b, ny) * nx + xh) for a, b in plane],
    ]
    slot = [q * nx + xh, z * ny + y]
    counts = [NQ * nx, nz * ny]

    barrier = pltpu.get_barrier_semaphore()
    beside = [(lax.rem(q + k, NQ), t) for k in range(NQ) for t in (up, down)]
    partners = phases[0] + beside + phases[1]
    for p in partners:
        pl.semaphore_signal(barrier, inc=1, device_id=p, device_id_type=MESH)

    base = pl.multiple_of(q * LANES, LANES)
    own = pl.ds(base, LANES)
    ins = [
        pltpu.make_async_copy(depth_hbm, depth, in_sem.at[0]),
        pltpu.make_async_copy(albedo_hbm, albedo, in_sem.at[1]),
        pltpu.make_async_copy(mask_hbm, mask, in_sem.at[2]),
        pltpu.make_async_copy(obs_hbm, obs_own, in_sem.at[3]),
    ]
    mine = pl.ds(pl.multiple_of(q * nl, nl), nl)

    def block(t, u):
        r = pl.ds(pl.multiple_of(u * UNIT, UNIT), UNIT)
        return obs_hbm.at[:, r, pl.ds(pl.multiple_of(t * LANES, LANES), LANES)]

    def stage(u, carry):
        for j, t in enumerate(others):
            pltpu.make_async_copy(block(t, u), staged.at[j, u], st_sem.at[j]).start()
        return carry

    def stage_own(u, carry):
        pltpu.make_async_copy(block(q, u), obs_all.at[u, mine], st_sem.at[NQ - 1]).start()
        return carry

    for c in ins[:3]:
        c.start()
    lax.fori_loop(0, nu, stage, 0)
    ins[3].start()
    lax.fori_loop(0, nu, stage_own, 0)

    def ob_copy(j, u):
        t = others[j]
        return remote(
            staged.at[j, u], obs_all.at[u, mine], ob_send.at[j, u], ob_recv.at[j, u], (t, s)
        )

    def send_obs(u, carry):
        for j in range(NQ - 1):
            ob_copy(j, u).start()
        return carry

    eye = lax.broadcasted_iota(jnp.int32, (rows, LANES), 0) == lax.broadcasted_iota(jnp.int32, (rows, LANES), 1)
    lane = lax.broadcasted_iota(jnp.int32, (rows, LANES), 1)
    lane1 = lax.broadcasted_iota(jnp.int32, (1, LANES), 1)

    def to_lanes(v, c):
        return jnp.sum(jnp.where(eye, jnp.broadcast_to(v[:, c : c + 1], (rows, LANES)), 0.0), axis=0, keepdims=True)

    def to_rows(v):
        return jnp.sum(jnp.where(eye, jnp.broadcast_to(v, (rows, LANES)), 0.0), axis=1, keepdims=True)

    def pack_edges(it, fields):
        k = 0
        for v, far in fields:
            pack_out[it, 0, k : k + 1, :] = to_lanes(v, LANES - 1)
            pack_out[it, 1, k : k + 1, :] = to_lanes(v, 0)
            k += 1
            if far:
                pack_out[it, 0, k : k + 1, :] = to_lanes(v, LANES - 2)
                pack_out[it, 1, k : k + 1, :] = to_lanes(v, 1)
                k += 1

    def send_edges(it):
        out = [
            remote(pack_out.at[it, 0], pack_in.at[it, 0], pk_send.at[it, 0], pk_recv.at[it, 0], right),
            remote(pack_out.at[it, 1], pack_in.at[it, 1], pk_send.at[it, 1], pk_recv.at[it, 1], left),
        ]
        for c in out:
            c.start()
        return out

    for k in range(3):
        ins[k].wait()
    center = pl.ds(8, rows)
    spad[...] = jnp.zeros_like(spad)
    gypad[...] = jnp.zeros_like(gypad)
    pack_out[...] = jnp.zeros_like(pack_out)
    spad[center, :] = depth[:, own]
    alb_own[...] = albedo[:, own]
    pack_edges(
        0, ((depth[:, own], True), (alb_own[...], False), (mask[:, own].astype(f32), False))
    )

    for k in range(4):
        row = jnp.zeros((1, LANES), f32)
        for l in range(nl):
            row = jnp.where(lane1 == l, table_ref[k, l].astype(f32), row)
        tables[pl.ds(q, 1), k : k + 1, :] = row[None]
    pl.semaphore_wait(barrier, len(partners))
    tb = [
        remote(tables.at[q], tables.at[q], tb_send.at[j], tb_recv.at[j], (t, s)) for j, t in enumerate(others)
    ]
    for c in tb:
        c.start()

    pk = send_edges(0)
    for j in range(NQ - 1):
        pltpu.make_async_copy(staged.at[j], staged.at[j], st_sem.at[j]).wait()
    lax.fori_loop(0, AHEAD, send_obs, 0)

    ins[3].wait()
    e_row = lax.broadcasted_iota(jnp.int32, (2 * NQ, COLS), 0)
    e_col = lax.broadcasted_iota(jnp.int32, (2 * NQ, COLS), 1)
    wanted = lax.rem((e_row // 2) * LANES + jnp.where(lax.rem(e_row, 2) == 0, COLS - 1, LANES), COLS)
    pick = jnp.where(e_col == wanted, 1.0, 0.0).astype(jnp.bfloat16)
    for l in range(nl):
        got = lax.dot_general(
            pick, obs_own[l], (((1,), (1,)), ((), ())), preferred_element_type=f32
        )
        for e in range(2 * NQ):
            edge_obs[e, l : l + 1, :] = got[e : e + 1]
    eo = []
    for j, t in enumerate(others):
        for side in range(2):
            strip = jnp.where(t == 0, up, s) if side == 0 else jnp.where(t == NQ - 1, down, s)
            eo.append(
                remote(
                    edge_obs.at[2 * t + side], halo_obs.at[side, mine],
                    eo_send.at[j, side], eo_recv.at[j, side], (t, strip),
                )
            )
    lo = [
        remote(edge_obs.at[0], halo_loop.at[0], lo_send.at[0], lo_recv.at[0], (q, up)),
        remote(edge_obs.at[2 * NQ - 1], halo_loop.at[1], lo_send.at[1], lo_recv.at[1], (q, down)),
    ]
    for c in eo + lo:
        c.start()

    lax.fori_loop(AHEAD, nu, send_obs, 0)

    for c in tb:
        c.wait()
    diagonal = lax.broadcasted_iota(jnp.int32, (nl, LANES), 0) == lax.broadcasted_iota(jnp.int32, (nl, LANES), 1)

    def component(k):
        return jnp.concatenate(
            [
                jnp.sum(jnp.where(diagonal, tables[g, k : k + 1, :], 0.0), axis=1, keepdims=True)
                for g in range(NQ)
            ],
            axis=0,
        )

    lx = component(0) / 500.0 - 1.0
    ly = component(1) / 500.0 - 1.0
    lz = 1.0 + component(2) / 1000.0
    le = 0.5 + component(3) / 1000.0
    for k, v in enumerate((lx, ly, lz, le)):
        lights[k] = jnp.broadcast_to(v, (NL, LANES))

    def coord_x(columns):
        return (columns.astype(f32) + 0.5) / TOTAL - 0.5

    def coord_y(index):
        return (index.astype(f32) + 0.5 - rows / 2.0) / TOTAL

    first = s * COLS + q * LANES
    px = coord_x(lane1 + first)
    py = coord_y(lax.broadcasted_iota(jnp.int32, (rows, LANES), 0))
    py_lane = coord_y(lane1)
    d = lx - px
    dx1[...] = d

    def make_c2(l, carry):
        dy = lights[1, pl.ds(l, 1), :] - py
        dxr = dx1[pl.ds(l, 1), :]
        dy1[l] = jnp.broadcast_to(dy, (rows, LANES))
        c2[l] = dy * dy + dxr * dxr
        return carry

    lax.fori_loop(0, NL, make_c2, 0)

    not_left = jnp.where((s == 0) & (q == 0), 0.0, 1.0).astype(f32)
    not_right = jnp.where((s == NS - 1) & (q == NQ - 1), 0.0, 1.0).astype(f32)
    keep = (not_left, not_right)

    for c in pk + eo + lo:
        c.wait()
    for side in range(2):
        inner = edge_obs[2 * q + side]
        at_end = (q == 0) if side == 0 else (q == NQ - 1)
        halo_obs[side, mine, :] = jnp.where(at_end, halo_loop[side], inner)
        v = pack_in[0, side]
        halo[side, 0:2, :] = v[0:2] * keep[side]
        halo[side, 2:4, :] = v[2:4]
    pltpu.make_async_copy(obs_all.at[:, mine], obs_all.at[:, mine], st_sem.at[NQ - 1]).wait()

    def widen(v, lo_col, hi_col):
        lo_v = jnp.where(lane == 0, lo_col, pltpu.roll(v, 1, 1))
        hi_v = jnp.where(lane == LANES - 1, hi_col, pltpu.roll(v, LANES - 1, 1))
        return lo_v, hi_v

    def side_gradient(side):
        near, far, alb, val = (halo[side, k : k + 1, :] for k in range(4))
        surf = spad[center, :]
        inside = to_lanes(surf, 0 if side == 0 else LANES - 1)
        sx = 0.5 * (inside - far) if side == 0 else 0.5 * (far - inside)
        below = jnp.where(lane1 == LANES - 1, 0.0, pltpu.roll(near, LANES - 1, 1))
        above = jnp.where(lane1 == 0, 0.0, pltpu.roll(near, 1, 1))
        sy = 0.5 * (below - above)
        nsq = 1.0 + sx * sx + sy * sy
        rn = lax.rsqrt(nsq)
        pxs = coord_x(jnp.full((1, LANES), first, jnp.int32) + (-1 if side == 0 else LANES))
        lxs, lys, lzs, les = (lights[k] for k in range(4))
        dx, dy, dz = lxs - pxs, lys - py_lane, lzs - near
        dist = dx * dx + dy * dy + dz * dz
        facing = dz - sx * dx - sy * dy
        ri = lax.rsqrt(dist)
        fall = les * (ri * ri * ri)
        t = (alb * rn) * (fall * facing) - halo_obs[side]
        uu = t * t
        p = jnp.exp2(HALF_LOG2E * (jnp.min(uu, axis=0, keepdims=True) - uu))
        pull = p * t * fall
        total = jnp.sum(p, axis=0, keepdims=True)
        inner = jnp.sum(pull * dx, axis=0, keepdims=True) + (sx * rn * rn) * jnp.sum(
            pull * facing, axis=0, keepdims=True
        )
        return to_rows(-(keep[side] * val * rn * alb / total) * inner)

    def drain(u, carry):
        for j in range(NQ - 1):
            ob_copy(j, u).wait_send()
        return carry

    sent, gathered = [], []
    for it in range(ITERS):
        last = it == ITERS - 1
        surf = spad[center, :]
        lo_v, hi_v = widen(surf, to_rows(halo[0, 0:1, :]), to_rows(halo[1, 0:1, :]))
        sx = 0.5 * (hi_v - lo_v)
        sy = 0.5 * (spad[pl.ds(9, rows), :] - spad[pl.ds(7, rows), :])
        nsq = 1.0 + sx * sx + sy * sy
        rn = lax.rsqrt(nsq)
        pix[0] = surf
        pix[2] = sx
        pix[3] = sy
        pix[4] = alb_own[...] * (rn * ROOT)
        pix[5] = mask[:, own].astype(f32) * (rn / ROOT)
        pix[6] = rn * rn
        gx_lo, gx_hi = side_gradient(0), side_gradient(1)

        def unit(u, carry):
            rs = pl.ds(pl.multiple_of(u * UNIT, UNIT), UNIT)
            if it == 0:
                for j in range(NQ - 1):
                    ob_copy(j, u).wait_recv()
            sv, sxv, syv, av = (pix[k, rs, :] for k in (0, 2, 3, 4))
            low = None
            for l in range(NL):
                ls = pl.ds(l, 1)
                lzv, lev = lights[2, ls, :], lights[3, ls, :]
                dz = lzv - sv
                dist = dz * dz + c2[l, rs, :]
                facing = dz - sxv * dx1[ls, :] - syv * dy1[l, rs, :]
                ri = lax.rsqrt(dist)
                r2 = ri * ri
                fall = lev * (r2 * ri)
                fac = fall * facing
                if it == 0:
                    seen = obs_all[u, l].astype(f32) * ROOT
                    obs_f[u, l] = seen
                else:
                    seen = obs_f[u, l]
                t = av * fac - seen
                tt[l] = t
                ff[l] = fall
                fp[l] = fac
                gg[l] = dz * r2
                uu = t * t
                low = uu if low is None else jnp.minimum(low, uu)
            acc = None
            for l in range(NL):
                ls = pl.ds(l, 1)
                t = tt[l]
                p = jnp.exp2(low - t * t)
                w = p * t
                pull = w * ff[l]
                pf = w * fp[l]
                new = (p, pf, pf * gg[l], pull, pull * dx1[ls, :], pull * dy1[l, rs, :])
                acc = new if acc is None else tuple(a + b for a, b in zip(acc, new))
            ssum, A, D, PU, X, Y = acc
            scale = pix[5, rs, :] / ssum
            alb = alb_own[rs, :]
            ga = scale * A
            ca = scale * alb
            tilt = ga * alb * pix[6, rs, :]
            ga_all[it, rs, own] = ga
            gd[rs, :] = ca * (3.0 * D - PU)
            gx[rs, :] = -ca * X - tilt * sxv
            gypad[pl.ds(pl.multiple_of(u * UNIT + 8, 8), UNIT), :] = -ca * Y - tilt * syv
            return carry

        lax.fori_loop(0, nu, unit, 0)
        lo_v, hi_v = widen(gx[...], gx_lo, gx_hi)
        fd = gd[...] + 0.5 * (lo_v - hi_v) + 0.5 * (gypad[pl.ds(7, rows), :] - gypad[pl.ds(9, rows), :])
        ga = ga_all[it, :, own]
        total = jnp.concatenate(
            [jnp.sum(fd * fd, axis=0, keepdims=True), jnp.sum(ga * ga, axis=0, keepdims=True)], axis=0
        )
        for k, sums in enumerate((near_sums, far_sums)):
            sums[it, pl.ds(slot[k], 1)] = total[None]
            part = sums.at[it, slot[k]]
            for p in phases[k]:
                remote(part, part, ar_send.at[it, k], ar_recv.at[it, k], p).start()
            if k == 0:
                fd_all[it, :, own] = fd
                theirs = pl.ds(pl.multiple_of((q ^ 2) * LANES, LANES), LANES)

                def moves(n, cols, device):
                    return [
                        remote(
                            ref.at[it, :, cols], ref.at[it, :, cols], fd_send.at[it, n, m], fd_recv.at[it, n, m], device
                        )
                        for m, ref in enumerate((fd_all, ga_all))
                    ]

                over, to_mate, onward = moves(0, own, across), moves(1, own, mate), moves(2, theirs, mate)
                if not last:
                    pack_edges(1, ((fd, True), (ga, False)))
                    pk = send_edges(1)
                for c in over + to_mate:
                    c.start()
            else:
                for c in over:
                    c.wait()
                for c in onward:
                    c.start()
                if not last:
                    lax.fori_loop(0, nu, drain, 0)
                if last:
                    for w in sent[:-1]:
                        w.wait_send()
                    for c in gathered:
                        c.wait()
                    depth[...] = depth[...] - step_depth * jnp.tanh(fd_all[0] * inv_d)
                    albedo[...] = albedo[...] - step_albedo * jnp.tanh(ga_all[0] * inv_a)
            whole = sums.at[it, pl.ds(0, counts[k] - 1)]
            w = remote(whole, whole, ar_send.at[it, k], ar_recv.at[it, k], phases[k][0])
            w.wait_recv()
            sent.append(w)
            total = jnp.sum(sums[it], axis=0)
        means = jnp.sum(total, axis=1, keepdims=True) / (rows * float(TOTAL))
        inv = 1.0 / jnp.sqrt(means + epsilon)
        inv_d, inv_a = inv[0:1, 0:1], inv[1:2, 0:1]
        if last:
            for c in to_mate + onward:
                c.wait()
            depth_out[...] = depth[...] - step_depth * jnp.tanh(fd_all[it] * inv_d)
            albedo_out[...] = albedo[...] - step_albedo * jnp.tanh(ga_all[it] * inv_a)
        else:
            gathered = to_mate + onward
            spad[center, :] = spad[center, :] - step_depth * jnp.tanh(fd_all[it, :, own] * inv_d)
            alb_own[...] = alb_own[...] - step_albedo * jnp.tanh(ga_all[it, :, own] * inv_a)
            for c in pk:
                c.wait()
            for side in range(2):
                v = pack_in[1, side]
                halo[side, 0:2, :] = keep[side] * (halo[side, 0:2, :] - step_depth * jnp.tanh(v[0:2] * inv_d))
                halo[side, 2:3, :] = halo[side, 2:3, :] - step_albedo * jnp.tanh(v[2:3] * inv_a)

    for w in sent[-2:]:
        w.wait_send()


def factors(n):
    return {128: (8, 8, 2)}[n]


def solution(mesh):
    NQ, NS = mesh.shape["light"], mesh.shape["strip"]

    def shards(depth, albedo, obs, table, mask):
        rows, cols = depth.shape
        nl = obs.shape[0]
        FACT = factors(NS)
        NL = NQ * nl
        nu = rows // UNIT
        cfg = (NQ, NS, cols, cols * NS, FACT)
        V, D = pltpu.VMEM, pltpu.SemaphoreType.DMA
        any_spec = pl.BlockSpec(memory_space=pl.ANY)
        vm = pl.BlockSpec(memory_space=pltpu.VMEM)
        out = jax.ShapeDtypeStruct((rows, cols), f32)
        return pl.pallas_call(
            functools.partial(kernel, cfg),
            out_shape=(out, out),
            in_specs=[any_spec] * 3 + [pl.BlockSpec(memory_space=pltpu.SMEM), any_spec],
            out_specs=(vm, vm),
            scratch_shapes=[
                V((rows, cols), f32), V((rows, cols), f32), V((rows, cols), jnp.int32),
                V((nl, rows, cols), jnp.bfloat16), V((nu, NL, UNIT, LANES), jnp.bfloat16),
                V((NQ, 4, LANES), f32), V((4, NL, LANES), f32),
                V((NQ - 1, nu, nl, UNIT, LANES), jnp.bfloat16),
                V((NL, LANES), f32), V((NL, rows, LANES), f32), V((nu, NL, UNIT, LANES), f32),
                V((NL, rows, LANES), f32), V((rows + 16, LANES), f32), V((rows, LANES), f32),
                V((rows, LANES), f32), V((rows + 16, LANES), f32), V((rows, LANES), f32), V((7, rows, LANES), f32),
                V((NL, UNIT, LANES), f32), V((NL, UNIT, LANES), f32),
                V((NL, UNIT, LANES), f32), V((NL, UNIT, LANES), f32),
                V((2 * NQ, nl, LANES), f32), V((2, NL, LANES), f32), V((2, nl, LANES), f32),
                V((ITERS, 2, 8, LANES), f32), V((ITERS, 2, 8, LANES), f32), V((2, 8, LANES), f32),
                V((ITERS, rows, cols), f32), V((ITERS, rows, cols), f32),
                V((ITERS, NQ * FACT[2], 2, LANES), f32), V((ITERS, FACT[0] * FACT[1], 2, LANES), f32),
                D((4,)), D((NQ,)), D((NQ - 1, nu)), D((NQ - 1, nu)), D((NQ - 1,)), D((NQ - 1,)),
                D((NQ - 1, 2)), D((NQ - 1, 2)), D((2,)), D((2,)),
                D((ITERS, 2)), D((ITERS, 2)), D((ITERS, 3, 2)), D((ITERS, 3, 2)), D((ITERS, 2)), D((ITERS, 2)),
            ],
            compiler_params=pltpu.CompilerParams(
                collective_id=0, has_side_effects=True, vmem_limit_bytes=40 * 2**20
            ),
            cost_estimate=pl.CostEstimate(flops=10**8, bytes_accessed=3 * 2**20, transcendentals=10**6),
            name="steps",
        )(*(pltpu.with_memory_space_constraint(v, pltpu.HBM) for v in (depth, albedo, obs, table.T, mask)))

    in_specs = (
        P(None, "strip"),
        P(None, "strip"),
        P("light", None, "strip"),
        P("light", None),
        P(None, "strip"),
    )
    return jax.shard_map(
        shards, mesh=mesh, in_specs=in_specs, out_specs=(P(None, "strip"), P(None, "strip")), check_vma=False
    )
```

```python
import functools

import jax
import jax.numpy as jnp
from jax import lax
from jax.experimental import pallas as pl
from jax.experimental.pallas import tpu as pltpu
from jax.sharding import PartitionSpec as P

MESH = pl.DeviceIdType.MESH
ITERS = 2
step_depth = 0.1
step_albedo = 0.2
epsilon = 1e-06
HALF_LOG2E = 0.5 * 1.4426950408889634
ROOT = HALF_LOG2E ** 0.5

UNIT = 16
AHEAD = 3
LANES = 128
f32 = jnp.float32


def remote(src, dst, send, recv, device):
    return pltpu.make_async_remote_copy(
        src_ref=src, dst_ref=dst, send_sem=send, recv_sem=recv, device_id=device, device_id_type=MESH
    )


def kernel(
    cfg,
    depth_hbm, albedo_hbm, obs_hbm, table_ref, mask_hbm,
    depth_out, albedo_out,
    depth, albedo, mask, obs_own, obs_all, tables, lights,
    staged, dx1, dy1, obs_f, c2, spad, alb_own, gx, gypad, gd, pix,
    tt, ff, fp, gg,
    edge_obs, halo_obs, halo_loop, pack_out, pack_in, halo,
    fd_all, ga_all, near_sums, far_sums,
    in_sem, st_sem, ob_send, ob_recv, tb_send, tb_recv, eo_send, eo_recv, lo_send, lo_recv,
    pk_send, pk_recv, fd_send, fd_recv, ar_send, ar_recv,
):
    NQ, NS, COLS, TOTAL, FACT = cfg
    nl = obs_hbm.shape[0]
    rows = depth_hbm.shape[0]
    nu = rows // UNIT
    NL = NQ * nl
    q = lax.axis_index("light")
    s = lax.axis_index("strip")
    nz, ny, nx = FACT
    z, y, xh = s // (ny * nx), lax.rem(s, ny * nx) // nx, lax.rem(s, nx)
    up, down = lax.rem(s + 1, NS), lax.rem(s + NS - 1, NS)
    others = [lax.rem(q + k, NQ) for k in (2, 3, 1)]
    across, mate = (q ^ 2, s), (q ^ 1, s)
    right = (lax.rem(q + 1, NQ), jnp.where(q == NQ - 1, up, s))
    left = (lax.rem(q + NQ - 1, NQ), jnp.where(q == 0, down, s))

    def ring(k, n):
        return min(k, n - k)

    plane = sorted(
        [(a, b) for a in range(nz) for b in range(ny) if (a, b) != (0, 0)],
        key=lambda o: -(ring(o[0], nz) + ring(o[1], ny)),
    )
    phases = [
        [
            (lax.rem(q + k, NQ), z * (ny * nx) + y * nx + lax.rem(xh + h, nx))
            for h in reversed(range(nx))
            for k in (2, 3, 1, 0)
            if (h, k) != (0, 0)
        ],
        [(q, lax.rem(z + a, nz) * (ny * nx) + lax.rem(y + b, ny) * nx + xh) for a, b in plane],
    ]
    slot = [q * nx + xh, z * ny + y]
    counts = [NQ * nx, nz * ny]

    barrier = pltpu.get_barrier_semaphore()
    beside = [(lax.rem(q + k, NQ), t) for k in range(NQ) for t in (up, down)]
    partners = phases[0] + beside + phases[1]
    for p in partners:
        pl.semaphore_signal(barrier, inc=1, device_id=p, device_id_type=MESH)

    base = pl.multiple_of(q * LANES, LANES)
    own = pl.ds(base, LANES)
    ins = [
        pltpu.make_async_copy(depth_hbm, depth, in_sem.at[0]),
        pltpu.make_async_copy(albedo_hbm, albedo, in_sem.at[1]),
        pltpu.make_async_copy(mask_hbm, mask, in_sem.at[2]),
        pltpu.make_async_copy(obs_hbm, obs_own, in_sem.at[3]),
    ]
    mine = pl.ds(pl.multiple_of(q * nl, nl), nl)

    def block(t, u):
        r = pl.ds(pl.multiple_of(u * UNIT, UNIT), UNIT)
        return obs_hbm.at[:, r, pl.ds(pl.multiple_of(t * LANES, LANES), LANES)]

    def stage(u, carry):
        for j, t in enumerate(others):
            pltpu.make_async_copy(block(t, u), staged.at[j, u], st_sem.at[j]).start()
        return carry

    def stage_own(u, carry):
        pltpu.make_async_copy(block(q, u), obs_all.at[u, mine], st_sem.at[NQ - 1]).start()
        return carry

    for c in ins[:3]:
        c.start()
    lax.fori_loop(0, nu, stage, 0)
    ins[3].start()
    lax.fori_loop(0, nu, stage_own, 0)

    def ob_copy(j, u):
        t = others[j]
        return remote(
            staged.at[j, u], obs_all.at[u, mine], ob_send.at[j, u], ob_recv.at[j, u], (t, s)
        )

    def send_obs(u, carry):
        for j in range(NQ - 1):
            ob_copy(j, u).start()
        return carry

    eye = lax.broadcasted_iota(jnp.int32, (rows, LANES), 0) == lax.broadcasted_iota(jnp.int32, (rows, LANES), 1)
    lane = lax.broadcasted_iota(jnp.int32, (rows, LANES), 1)
    lane1 = lax.broadcasted_iota(jnp.int32, (1, LANES), 1)

    def to_lanes(v, c):
        return jnp.sum(jnp.where(eye, jnp.broadcast_to(v[:, c : c + 1], (rows, LANES)), 0.0), axis=0, keepdims=True)

    def to_rows(v):
        return jnp.sum(jnp.where(eye, jnp.broadcast_to(v, (rows, LANES)), 0.0), axis=1, keepdims=True)

    def pack_edges(it, fields):
        k = 0
        for v, far in fields:
            pack_out[it, 0, k : k + 1, :] = to_lanes(v, LANES - 1)
            pack_out[it, 1, k : k + 1, :] = to_lanes(v, 0)
            k += 1
            if far:
                pack_out[it, 0, k : k + 1, :] = to_lanes(v, LANES - 2)
                pack_out[it, 1, k : k + 1, :] = to_lanes(v, 1)
                k += 1

    def send_edges(it):
        out = [
            remote(pack_out.at[it, 0], pack_in.at[it, 0], pk_send.at[it, 0], pk_recv.at[it, 0], right),
            remote(pack_out.at[it, 1], pack_in.at[it, 1], pk_send.at[it, 1], pk_recv.at[it, 1], left),
        ]
        for c in out:
            c.start()
        return out

    for k in range(3):
        ins[k].wait()
    center = pl.ds(8, rows)
    spad[...] = jnp.zeros_like(spad)
    gypad[...] = jnp.zeros_like(gypad)
    pack_out[...] = jnp.zeros_like(pack_out)
    spad[center, :] = depth[:, own]
    alb_own[...] = albedo[:, own]
    pack_edges(
        0, ((depth[:, own], True), (alb_own[...], False), (mask[:, own].astype(f32), False))
    )

    for k in range(4):
        row = jnp.zeros((1, LANES), f32)
        for l in range(nl):
            row = jnp.where(lane1 == l, table_ref[k, l].astype(f32), row)
        tables[pl.ds(q, 1), k : k + 1, :] = row[None]
    pl.semaphore_wait(barrier, len(partners))
    tb = [
        remote(tables.at[q], tables.at[q], tb_send.at[j], tb_recv.at[j], (t, s)) for j, t in enumerate(others)
    ]
    for c in tb:
        c.start()

    pk = send_edges(0)
    for j in range(NQ - 1):
        pltpu.make_async_copy(staged.at[j], staged.at[j], st_sem.at[j]).wait()
    lax.fori_loop(0, AHEAD, send_obs, 0)

    ins[3].wait()
    e_row = lax.broadcasted_iota(jnp.int32, (2 * NQ, COLS), 0)
    e_col = lax.broadcasted_iota(jnp.int32, (2 * NQ, COLS), 1)
    wanted = lax.rem((e_row // 2) * LANES + jnp.where(lax.rem(e_row, 2) == 0, COLS - 1, LANES), COLS)
    pick = jnp.where(e_col == wanted, 1.0, 0.0).astype(jnp.bfloat16)
    for l in range(nl):
        got = lax.dot_general(
            pick, obs_own[l], (((1,), (1,)), ((), ())), preferred_element_type=f32
        )
        for e in range(2 * NQ):
            edge_obs[e, l : l + 1, :] = got[e : e + 1]
    eo = []
    for j, t in enumerate(others):
        for side in range(2):
            strip = jnp.where(t == 0, up, s) if side == 0 else jnp.where(t == NQ - 1, down, s)
            eo.append(
                remote(
                    edge_obs.at[2 * t + side], halo_obs.at[side, mine],
                    eo_send.at[j, side], eo_recv.at[j, side], (t, strip),
                )
            )
    lo = [
        remote(edge_obs.at[0], halo_loop.at[0], lo_send.at[0], lo_recv.at[0], (q, up)),
        remote(edge_obs.at[2 * NQ - 1], halo_loop.at[1], lo_send.at[1], lo_recv.at[1], (q, down)),
    ]
    for c in eo + lo:
        c.start()

    lax.fori_loop(AHEAD, nu, send_obs, 0)

    for c in tb:
        c.wait()
    diagonal = lax.broadcasted_iota(jnp.int32, (nl, LANES), 0) == lax.broadcasted_iota(jnp.int32, (nl, LANES), 1)

    def component(k):
        return jnp.concatenate(
            [
                jnp.sum(jnp.where(diagonal, tables[g, k : k + 1, :], 0.0), axis=1, keepdims=True)
                for g in range(NQ)
            ],
            axis=0,
        )

    lx = component(0) / 500.0 - 1.0
    ly = component(1) / 500.0 - 1.0
    lz = 1.0 + component(2) / 1000.0
    le = 0.5 + component(3) / 1000.0
    for k, v in enumerate((lx, ly, lz, le)):
        lights[k] = jnp.broadcast_to(v, (NL, LANES))

    def coord_x(columns):
        return (columns.astype(f32) + 0.5) / TOTAL - 0.5

    def coord_y(index):
        return (index.astype(f32) + 0.5 - rows / 2.0) / TOTAL

    first = s * COLS + q * LANES
    px = coord_x(lane1 + first)
    py = coord_y(lax.broadcasted_iota(jnp.int32, (rows, LANES), 0))
    py_lane = coord_y(lane1)
    d = lx - px
    dx1[...] = d

    def make_c2(l, carry):
        dy = lights[1, pl.ds(l, 1), :] - py
        dxr = dx1[pl.ds(l, 1), :]
        dy1[l] = jnp.broadcast_to(dy, (rows, LANES))
        c2[l] = dy * dy + dxr * dxr
        return carry

    lax.fori_loop(0, NL, make_c2, 0)

    not_left = jnp.where((s == 0) & (q == 0), 0.0, 1.0).astype(f32)
    not_right = jnp.where((s == NS - 1) & (q == NQ - 1), 0.0, 1.0).astype(f32)
    keep = (not_left, not_right)

    for c in pk + eo + lo:
        c.wait()
    for side in range(2):
        inner = edge_obs[2 * q + side]
        at_end = (q == 0) if side == 0 else (q == NQ - 1)
        halo_obs[side, mine, :] = jnp.where(at_end, halo_loop[side], inner)
        v = pack_in[0, side]
        halo[side, 0:2, :] = v[0:2] * keep[side]
        halo[side, 2:4, :] = v[2:4]
    pltpu.make_async_copy(obs_all.at[:, mine], obs_all.at[:, mine], st_sem.at[NQ - 1]).wait()

    def widen(v, lo_col, hi_col):
        lo_v = jnp.where(lane == 0, lo_col, pltpu.roll(v, 1, 1))
        hi_v = jnp.where(lane == LANES - 1, hi_col, pltpu.roll(v, LANES - 1, 1))
        return lo_v, hi_v

    def side_gradient(side):
        near, far, alb, val = (halo[side, k : k + 1, :] for k in range(4))
        surf = spad[center, :]
        inside = to_lanes(surf, 0 if side == 0 else LANES - 1)
        sx = 0.5 * (inside - far) if side == 0 else 0.5 * (far - inside)
        below = jnp.where(lane1 == LANES - 1, 0.0, pltpu.roll(near, LANES - 1, 1))
        above = jnp.where(lane1 == 0, 0.0, pltpu.roll(near, 1, 1))
        sy = 0.5 * (below - above)
        nsq = 1.0 + sx * sx + sy * sy
        rn = lax.rsqrt(nsq)
        pxs = coord_x(jnp.full((1, LANES), first, jnp.int32) + (-1 if side == 0 else LANES))
        lxs, lys, lzs, les = (lights[k] for k in range(4))
        dx, dy, dz = lxs - pxs, lys - py_lane, lzs - near
        dist = dx * dx + dy * dy + dz * dz
        facing = dz - sx * dx - sy * dy
        ri = lax.rsqrt(dist)
        fall = les * (ri * ri * ri)
        t = (alb * rn) * (fall * facing) - halo_obs[side]
        uu = t * t
        p = jnp.exp2(HALF_LOG2E * (jnp.min(uu, axis=0, keepdims=True) - uu))
        pull = p * t * fall
        total = jnp.sum(p, axis=0, keepdims=True)
        inner = jnp.sum(pull * dx, axis=0, keepdims=True) + (sx * rn * rn) * jnp.sum(
            pull * facing, axis=0, keepdims=True
        )
        return to_rows(-(keep[side] * val * rn * alb / total) * inner)

    def drain(u, carry):
        for j in range(NQ - 1):
            ob_copy(j, u).wait_send()
        return carry

    sent, gathered = [], []
    for it in range(ITERS):
        last = it == ITERS - 1
        surf = spad[center, :]
        lo_v, hi_v = widen(surf, to_rows(halo[0, 0:1, :]), to_rows(halo[1, 0:1, :]))
        sx = 0.5 * (hi_v - lo_v)
        sy = 0.5 * (spad[pl.ds(9, rows), :] - spad[pl.ds(7, rows), :])
        nsq = 1.0 + sx * sx + sy * sy
        rn = lax.rsqrt(nsq)
        pix[0] = surf
        pix[2] = sx
        pix[3] = sy
        pix[4] = alb_own[...] * (rn * ROOT)
        pix[5] = mask[:, own].astype(f32) * (rn / ROOT)
        pix[6] = rn * rn
        gx_lo, gx_hi = side_gradient(0), side_gradient(1)

        def unit(u, carry):
            rs = pl.ds(pl.multiple_of(u * UNIT, UNIT), UNIT)
            if it == 0:
                for j in range(NQ - 1):
                    ob_copy(j, u).wait_recv()
            sv, sxv, syv, av = (pix[k, rs, :] for k in (0, 2, 3, 4))
            low = None
            for l in range(NL):
                ls = pl.ds(l, 1)
                lzv, lev = lights[2, ls, :], lights[3, ls, :]
                dz = lzv - sv
                dist = dz * dz + c2[l, rs, :]
                facing = dz - sxv * dx1[ls, :] - syv * dy1[l, rs, :]
                ri = lax.rsqrt(dist)
                r2 = ri * ri
                fall = lev * (r2 * ri)
                fac = fall * facing
                if it == 0:
                    seen = obs_all[u, l].astype(f32) * ROOT
                    obs_f[u, l] = seen
                else:
                    seen = obs_f[u, l]
                t = av * fac - seen
                tt[l] = t
                ff[l] = fall
                fp[l] = fac
                gg[l] = dz * r2
                uu = t * t
                low = uu if low is None else jnp.minimum(low, uu)
            acc = None
            for l in range(NL):
                ls = pl.ds(l, 1)
                t = tt[l]
                p = jnp.exp2(low - t * t)
                w = p * t
                pull = w * ff[l]
                pf = w * fp[l]
                new = (p, pf, pf * gg[l], pull, pull * dx1[ls, :], pull * dy1[l, rs, :])
                acc = new if acc is None else tuple(a + b for a, b in zip(acc, new))
            ssum, A, D, PU, X, Y = acc
            scale = pix[5, rs, :] / ssum
            alb = alb_own[rs, :]
            ga = scale * A
            ca = scale * alb
            tilt = ga * alb * pix[6, rs, :]
            ga_all[it, rs, own] = ga
            gd[rs, :] = ca * (3.0 * D - PU)
            gx[rs, :] = -ca * X - tilt * sxv
            gypad[pl.ds(pl.multiple_of(u * UNIT + 8, 8), UNIT), :] = -ca * Y - tilt * syv
            return carry

        lax.fori_loop(0, nu, unit, 0)
        lo_v, hi_v = widen(gx[...], gx_lo, gx_hi)
        fd = gd[...] + 0.5 * (lo_v - hi_v) + 0.5 * (gypad[pl.ds(7, rows), :] - gypad[pl.ds(9, rows), :])
        ga = ga_all[it, :, own]
        total = jnp.concatenate(
            [jnp.sum(fd * fd, axis=0, keepdims=True), jnp.sum(ga * ga, axis=0, keepdims=True)], axis=0
        )
        for k, sums in enumerate((near_sums, far_sums)):
            sums[it, pl.ds(slot[k], 1)] = total[None]
            part = sums.at[it, slot[k]]
            for p in phases[k]:
                remote(part, part, ar_send.at[it, k], ar_recv.at[it, k], p).start()
            if k == 0:
                fd_all[it, :, own] = fd
                theirs = pl.ds(pl.multiple_of((q ^ 2) * LANES, LANES), LANES)

                def moves(n, cols, device):
                    return [
                        remote(
                            ref.at[it, :, cols], ref.at[it, :, cols], fd_send.at[it, n, m], fd_recv.at[it, n, m], device
                        )
                        for m, ref in enumerate((fd_all, ga_all))
                    ]

                over, to_mate, onward = moves(0, own, across), moves(1, own, mate), moves(2, theirs, mate)
                if not last:
                    pack_edges(1, ((fd, True), (ga, False)))
                    pk = send_edges(1)
                for c in over + to_mate:
                    c.start()
            else:
                for c in over:
                    c.wait()
                for c in onward:
                    c.start()
                if not last:
                    lax.fori_loop(0, nu, drain, 0)
                if last:
                    for w in sent[:-1]:
                        w.wait_send()
                    for c in gathered:
                        c.wait()
                    depth[...] = depth[...] - step_depth * jnp.tanh(fd_all[0] * inv_d)
                    albedo[...] = albedo[...] - step_albedo * jnp.tanh(ga_all[0] * inv_a)
            whole = sums.at[it, pl.ds(0, counts[k] - 1)]
            w = remote(whole, whole, ar_send.at[it, k], ar_recv.at[it, k], phases[k][0])
            w.wait_recv()
            sent.append(w)
            total = jnp.sum(sums[it], axis=0)
        means = jnp.sum(total, axis=1, keepdims=True) / (rows * float(TOTAL))
        inv = 1.0 / jnp.sqrt(means + epsilon)
        inv_d, inv_a = inv[0:1, 0:1], inv[1:2, 0:1]
        if last:
            for c in to_mate + onward:
                c.wait()
            depth_out[...] = depth[...] - step_depth * jnp.tanh(fd_all[it] * inv_d)
            albedo_out[...] = albedo[...] - step_albedo * jnp.tanh(ga_all[it] * inv_a)
        else:
            gathered = to_mate + onward
            spad[center, :] = spad[center, :] - step_depth * jnp.tanh(fd_all[it, :, own] * inv_d)
            alb_own[...] = alb_own[...] - step_albedo * jnp.tanh(ga_all[it, :, own] * inv_a)
            for c in pk:
                c.wait()
            for side in range(2):
                v = pack_in[1, side]
                halo[side, 0:2, :] = keep[side] * (halo[side, 0:2, :] - step_depth * jnp.tanh(v[0:2] * inv_d))
                halo[side, 2:3, :] = halo[side, 2:3, :] - step_albedo * jnp.tanh(v[2:3] * inv_a)

    for w in sent[-2:]:
        w.wait_send()


def write_out(depth_in, albedo_in, depth_hbm, albedo_hbm, sem):
    copies = [
        pltpu.make_async_copy(depth_in, depth_hbm, sem.at[0]),
        pltpu.make_async_copy(albedo_in, albedo_hbm, sem.at[1]),
    ]
    for c in copies:
        c.start()
    for c in copies:
        c.wait()


def factors(n):
    return {128: (8, 8, 2)}[n]


def solution(mesh):
    NQ, NS = mesh.shape["light"], mesh.shape["strip"]

    def shards(depth, albedo, obs, table, mask):
        rows, cols = depth.shape
        nl = obs.shape[0]
        FACT = factors(NS)
        NL = NQ * nl
        nu = rows // UNIT
        cfg = (NQ, NS, cols, cols * NS, FACT)
        V, D = pltpu.VMEM, pltpu.SemaphoreType.DMA
        any_spec = pl.BlockSpec(memory_space=pl.ANY)
        vm = pl.BlockSpec(memory_space=pltpu.VMEM)
        out = jax.ShapeDtypeStruct((rows, cols), f32)
        results = pl.pallas_call(
            functools.partial(kernel, cfg),
            out_shape=(out, out),
            in_specs=[any_spec] * 3 + [pl.BlockSpec(memory_space=pltpu.SMEM), any_spec],
            out_specs=(vm, vm),
            scratch_shapes=[
                V((rows, cols), f32), V((rows, cols), f32), V((rows, cols), jnp.int32),
                V((nl, rows, cols), jnp.bfloat16), V((nu, NL, UNIT, LANES), jnp.bfloat16),
                V((NQ, 4, LANES), f32), V((4, NL, LANES), f32),
                V((NQ - 1, nu, nl, UNIT, LANES), jnp.bfloat16),
                V((NL, LANES), f32), V((NL, rows, LANES), f32), V((nu, NL, UNIT, LANES), f32),
                V((NL, rows, LANES), f32), V((rows + 16, LANES), f32), V((rows, LANES), f32),
                V((rows, LANES), f32), V((rows + 16, LANES), f32), V((rows, LANES), f32), V((7, rows, LANES), f32),
                V((NL, UNIT, LANES), f32), V((NL, UNIT, LANES), f32),
                V((NL, UNIT, LANES), f32), V((NL, UNIT, LANES), f32),
                V((2 * NQ, nl, LANES), f32), V((2, NL, LANES), f32), V((2, nl, LANES), f32),
                V((ITERS, 2, 8, LANES), f32), V((ITERS, 2, 8, LANES), f32), V((2, 8, LANES), f32),
                V((ITERS, rows, cols), f32), V((ITERS, rows, cols), f32),
                V((ITERS, NQ * FACT[2], 2, LANES), f32), V((ITERS, FACT[0] * FACT[1], 2, LANES), f32),
                D((4,)), D((NQ,)), D((NQ - 1, nu)), D((NQ - 1, nu)), D((NQ - 1,)), D((NQ - 1,)),
                D((NQ - 1, 2)), D((NQ - 1, 2)), D((2,)), D((2,)),
                D((ITERS, 2)), D((ITERS, 2)), D((ITERS, 3, 2)), D((ITERS, 3, 2)), D((ITERS, 2)), D((ITERS, 2)),
            ],
            compiler_params=pltpu.CompilerParams(
                collective_id=0, has_side_effects=True, vmem_limit_bytes=40 * 2**20
            ),
            cost_estimate=pl.CostEstimate(flops=10**8, bytes_accessed=3 * 2**20, transcendentals=10**6),
            name="steps",
        )(*(pltpu.with_memory_space_constraint(v, pltpu.HBM) for v in (depth, albedo, obs, table.T, mask)))
        return pl.pallas_call(
            write_out,
            out_shape=(out, out),
            in_specs=[vm, vm],
            out_specs=(pl.BlockSpec(memory_space=pltpu.HBM),) * 2,
            scratch_shapes=[D((2,))],
            compiler_params=pltpu.CompilerParams(vmem_limit_bytes=16 * 2**20),
            name="write_out",
        )(*results)

    in_specs = (
        P(None, "strip"),
        P(None, "strip"),
        P("light", None, "strip"),
        P("light", None),
        P(None, "strip"),
    )
    return jax.shard_map(
        shards, mesh=mesh, in_specs=in_specs, out_specs=(P(None, "strip"), P(None, "strip")), check_vma=False
    )
```

```python
import functools

import jax
import jax.numpy as jnp
from jax import lax
from jax.experimental import pallas as pl
from jax.experimental.pallas import tpu as pltpu
from jax.sharding import PartitionSpec as P

MESH = pl.DeviceIdType.MESH
ITERS = 2
step_depth = 0.1
step_albedo = 0.2
epsilon = 1e-06
HALF_LOG2E = 0.5 * 1.4426950408889634
ROOT = HALF_LOG2E ** 0.5

UNIT = 16
AHEAD = 3
LANES = 128
f32 = jnp.float32


def remote(src, dst, send, recv, device):
    return pltpu.make_async_remote_copy(
        src_ref=src, dst_ref=dst, send_sem=send, recv_sem=recv, device_id=device, device_id_type=MESH
    )


def kernel(
    cfg,
    depth_hbm, albedo_hbm, obs_hbm, table_ref, mask_hbm,
    depth_out, albedo_out,
    depth, albedo, mask, obs_own, obs_all, tables, lights,
    dx1, dy1, obs_f, c2, spad, alb_own, gx, gypad, gd, pix,
    tt, ff, fp, gg,
    edge_obs, halo_obs, halo_loop, pack_out, pack_in, halo,
    fd_all, ga_all, near_sums, far_sums,
    in_sem, st_sem, ob_send, ob_recv, tb_send, tb_recv, eo_send, eo_recv, lo_send, lo_recv,
    pk_send, pk_recv, fd_send, fd_recv, ar_send, ar_recv,
):
    NQ, NS, COLS, TOTAL, FACT = cfg
    nl = obs_hbm.shape[0]
    rows = depth_hbm.shape[0]
    nu = rows // UNIT
    NL = NQ * nl
    q = lax.axis_index("light")
    s = lax.axis_index("strip")
    nz, ny, nx = FACT
    z, y, xh = s // (ny * nx), lax.rem(s, ny * nx) // nx, lax.rem(s, nx)
    up, down = lax.rem(s + 1, NS), lax.rem(s + NS - 1, NS)
    others = [lax.rem(q + k, NQ) for k in (2, 3, 1)]
    across, mate = (q ^ 2, s), (q ^ 1, s)
    right = (lax.rem(q + 1, NQ), jnp.where(q == NQ - 1, up, s))
    left = (lax.rem(q + NQ - 1, NQ), jnp.where(q == 0, down, s))

    def ring(k, n):
        return min(k, n - k)

    plane = sorted(
        [(a, b) for a in range(nz) for b in range(ny) if (a, b) != (0, 0)],
        key=lambda o: -(ring(o[0], nz) + ring(o[1], ny)),
    )
    phases = [
        [
            (lax.rem(q + k, NQ), z * (ny * nx) + y * nx + lax.rem(xh + h, nx))
            for h in reversed(range(nx))
            for k in (2, 3, 1, 0)
            if (h, k) != (0, 0)
        ],
        [(q, lax.rem(z + a, nz) * (ny * nx) + lax.rem(y + b, ny) * nx + xh) for a, b in plane],
    ]
    slot = [q * nx + xh, z * ny + y]
    counts = [NQ * nx, nz * ny]

    barrier = pltpu.get_barrier_semaphore()
    other = jnp.where(xh == 0, down, up)
    beside = [(lax.rem(q + k, NQ), other) for k in range(NQ)]
    partners = phases[0] + beside + phases[1]
    for p in partners:
        pl.semaphore_signal(barrier, inc=1, device_id=p, device_id_type=MESH)

    base = pl.multiple_of(q * LANES, LANES)
    own = pl.ds(base, LANES)
    ins = [
        pltpu.make_async_copy(depth_hbm, depth, in_sem.at[0]),
        pltpu.make_async_copy(albedo_hbm, albedo, in_sem.at[1]),
        pltpu.make_async_copy(mask_hbm, mask, in_sem.at[2]),
        pltpu.make_async_copy(obs_hbm, obs_own, in_sem.at[3]),
    ]
    mine = pl.ds(pl.multiple_of(q * nl, nl), nl)

    def block(t, u):
        r = pl.ds(pl.multiple_of(u * UNIT, UNIT), UNIT)
        return obs_hbm.at[:, r, pl.ds(pl.multiple_of(t * LANES, LANES), LANES)]

    def stage_own(u, carry):
        pltpu.make_async_copy(block(q, u), obs_all.at[u, mine], st_sem.at[0]).start()
        return carry

    for c in ins[:3]:
        c.start()
    ins[3].start()
    lax.fori_loop(0, nu, stage_own, 0)

    def ob_copy(j, u):
        t = others[j]
        return remote(
            block(others[j], u), obs_all.at[u, mine], ob_send.at[j, u], ob_recv.at[j, u], (t, s)
        )

    def send_obs(u, carry):
        for j in range(NQ - 1):
            ob_copy(j, u).start()
        return carry

    eye = lax.broadcasted_iota(jnp.int32, (rows, LANES), 0) == lax.broadcasted_iota(jnp.int32, (rows, LANES), 1)
    lane = lax.broadcasted_iota(jnp.int32, (rows, LANES), 1)
    lane1 = lax.broadcasted_iota(jnp.int32, (1, LANES), 1)

    def to_lanes(v, c):
        return jnp.sum(jnp.where(eye, jnp.broadcast_to(v[:, c : c + 1], (rows, LANES)), 0.0), axis=0, keepdims=True)

    def to_rows(v):
        return jnp.sum(jnp.where(eye, jnp.broadcast_to(v, (rows, LANES)), 0.0), axis=1, keepdims=True)

    def pack_edges(it, fields):
        k = 0
        for v, far in fields:
            pack_out[it, 0, k : k + 1, :] = to_lanes(v, LANES - 1)
            pack_out[it, 1, k : k + 1, :] = to_lanes(v, 0)
            k += 1
            if far:
                pack_out[it, 0, k : k + 1, :] = to_lanes(v, LANES - 2)
                pack_out[it, 1, k : k + 1, :] = to_lanes(v, 1)
                k += 1

    def send_edges(it):
        out = [
            remote(pack_out.at[it, 0], pack_in.at[it, 0], pk_send.at[it, 0], pk_recv.at[it, 0], right),
            remote(pack_out.at[it, 1], pack_in.at[it, 1], pk_send.at[it, 1], pk_recv.at[it, 1], left),
        ]
        for c in out:
            c.start()
        return out

    for k in range(3):
        ins[k].wait()
    center = pl.ds(8, rows)
    spad[...] = jnp.zeros_like(spad)
    gypad[...] = jnp.zeros_like(gypad)
    pack_out[...] = jnp.zeros_like(pack_out)
    spad[center, :] = depth[:, own]
    alb_own[...] = albedo[:, own]
    pack_edges(
        0, ((depth[:, own], True), (alb_own[...], False), (mask[:, own].astype(f32), False))
    )

    for k in range(4):
        row = jnp.zeros((1, LANES), f32)
        for l in range(nl):
            row = jnp.where(lane1 == l, table_ref[k, l].astype(f32), row)
        tables[pl.ds(q, 1), k : k + 1, :] = row[None]
    pl.semaphore_wait(barrier, len(partners))
    tb = [
        remote(tables.at[q], tables.at[q], tb_send.at[j], tb_recv.at[j], (t, s)) for j, t in enumerate(others)
    ]
    for c in tb:
        c.start()

    pk = send_edges(0)
    lax.fori_loop(0, AHEAD, send_obs, 0)

    ins[3].wait()
    e_row = lax.broadcasted_iota(jnp.int32, (2 * NQ, COLS), 0)
    e_col = lax.broadcasted_iota(jnp.int32, (2 * NQ, COLS), 1)
    wanted = lax.rem((e_row // 2) * LANES + jnp.where(lax.rem(e_row, 2) == 0, COLS - 1, LANES), COLS)
    pick = jnp.where(e_col == wanted, 1.0, 0.0).astype(jnp.bfloat16)
    for l in range(nl):
        got = lax.dot_general(
            pick, obs_own[l], (((1,), (1,)), ((), ())), preferred_element_type=f32
        )
        for e in range(2 * NQ):
            edge_obs[e, l : l + 1, :] = got[e : e + 1]
    eo = []
    for j, t in enumerate(others):
        for side in range(2):
            strip = jnp.where(t == 0, up, s) if side == 0 else jnp.where(t == NQ - 1, down, s)
            eo.append(
                remote(
                    edge_obs.at[2 * t + side], halo_obs.at[side, mine],
                    eo_send.at[j, side], eo_recv.at[j, side], (t, strip),
                )
            )
    lo = [
        remote(edge_obs.at[0], halo_loop.at[0], lo_send.at[0], lo_recv.at[0], (q, up)),
        remote(edge_obs.at[2 * NQ - 1], halo_loop.at[1], lo_send.at[1], lo_recv.at[1], (q, down)),
    ]
    for c in eo + lo:
        c.start()

    lax.fori_loop(AHEAD, nu, send_obs, 0)

    for c in tb:
        c.wait()
    diagonal = lax.broadcasted_iota(jnp.int32, (nl, LANES), 0) == lax.broadcasted_iota(jnp.int32, (nl, LANES), 1)

    def component(k):
        return jnp.concatenate(
            [
                jnp.sum(jnp.where(diagonal, tables[g, k : k + 1, :], 0.0), axis=1, keepdims=True)
                for g in range(NQ)
            ],
            axis=0,
        )

    lx = component(0) / 500.0 - 1.0
    ly = component(1) / 500.0 - 1.0
    lz = 1.0 + component(2) / 1000.0
    le = 0.5 + component(3) / 1000.0
    for k, v in enumerate((lx, ly, lz, le)):
        lights[k] = jnp.broadcast_to(v, (NL, LANES))

    def coord_x(columns):
        return (columns.astype(f32) + 0.5) / TOTAL - 0.5

    def coord_y(index):
        return (index.astype(f32) + 0.5 - rows / 2.0) / TOTAL

    first = s * COLS + q * LANES
    px = coord_x(lane1 + first)
    py = coord_y(lax.broadcasted_iota(jnp.int32, (rows, LANES), 0))
    py_lane = coord_y(lane1)
    d = lx - px
    dx1[...] = d

    def make_c2(l, carry):
        dy = lights[1, pl.ds(l, 1), :] - py
        dxr = dx1[pl.ds(l, 1), :]
        dy1[l] = jnp.broadcast_to(dy, (rows, LANES))
        c2[l] = dy * dy + dxr * dxr
        return carry

    lax.fori_loop(0, NL, make_c2, 0)

    not_left = jnp.where((s == 0) & (q == 0), 0.0, 1.0).astype(f32)
    not_right = jnp.where((s == NS - 1) & (q == NQ - 1), 0.0, 1.0).astype(f32)
    keep = (not_left, not_right)

    for c in pk + eo + lo:
        c.wait()
    for side in range(2):
        inner = edge_obs[2 * q + side]
        at_end = (q == 0) if side == 0 else (q == NQ - 1)
        halo_obs[side, mine, :] = jnp.where(at_end, halo_loop[side], inner)
        v = pack_in[0, side]
        halo[side, 0:2, :] = v[0:2] * keep[side]
        halo[side, 2:4, :] = v[2:4]
    pltpu.make_async_copy(obs_all.at[:, mine], obs_all.at[:, mine], st_sem.at[0]).wait()

    def widen(v, lo_col, hi_col):
        lo_v = jnp.where(lane == 0, lo_col, pltpu.roll(v, 1, 1))
        hi_v = jnp.where(lane == LANES - 1, hi_col, pltpu.roll(v, LANES - 1, 1))
        return lo_v, hi_v

    def side_gradient(side):
        near, far, alb, val = (halo[side, k : k + 1, :] for k in range(4))
        surf = spad[center, :]
        inside = to_lanes(surf, 0 if side == 0 else LANES - 1)
        sx = 0.5 * (inside - far) if side == 0 else 0.5 * (far - inside)
        below = jnp.where(lane1 == LANES - 1, 0.0, pltpu.roll(near, LANES - 1, 1))
        above = jnp.where(lane1 == 0, 0.0, pltpu.roll(near, 1, 1))
        sy = 0.5 * (below - above)
        nsq = 1.0 + sx * sx + sy * sy
        rn = lax.rsqrt(nsq)
        pxs = coord_x(jnp.full((1, LANES), first, jnp.int32) + (-1 if side == 0 else LANES))
        lxs, lys, lzs, les = (lights[k] for k in range(4))
        dx, dy, dz = lxs - pxs, lys - py_lane, lzs - near
        dist = dx * dx + dy * dy + dz * dz
        facing = dz - sx * dx - sy * dy
        ri = lax.rsqrt(dist)
        fall = les * (ri * ri * ri)
        t = (alb * rn) * (fall * facing) - halo_obs[side]
        uu = t * t
        p = jnp.exp2(HALF_LOG2E * (jnp.min(uu, axis=0, keepdims=True) - uu))
        pull = p * t * fall
        total = jnp.sum(p, axis=0, keepdims=True)
        inner = jnp.sum(pull * dx, axis=0, keepdims=True) + (sx * rn * rn) * jnp.sum(
            pull * facing, axis=0, keepdims=True
        )
        return to_rows(-(keep[side] * val * rn * alb / total) * inner)

    def drain(u, carry):
        for j in range(NQ - 1):
            ob_copy(j, u).wait_send()
        return carry

    sent, gathered = [], []
    for it in range(ITERS):
        last = it == ITERS - 1
        surf = spad[center, :]
        lo_v, hi_v = widen(surf, to_rows(halo[0, 0:1, :]), to_rows(halo[1, 0:1, :]))
        sx = 0.5 * (hi_v - lo_v)
        sy = 0.5 * (spad[pl.ds(9, rows), :] - spad[pl.ds(7, rows), :])
        nsq = 1.0 + sx * sx + sy * sy
        rn = lax.rsqrt(nsq)
        pix[0] = surf
        pix[2] = sx
        pix[3] = sy
        pix[4] = alb_own[...] * (rn * ROOT)
        pix[5] = mask[:, own].astype(f32) * (rn / ROOT)
        pix[6] = rn * rn
        if it == 0:
            gx_lo, gx_hi = side_gradient(0), side_gradient(1)

        def unit(u, carry):
            rs = pl.ds(pl.multiple_of(u * UNIT, UNIT), UNIT)
            if it == 0:
                for j in range(NQ - 1):
                    ob_copy(j, u).wait_recv()
            sv, sxv, syv, av = (pix[k, rs, :] for k in (0, 2, 3, 4))
            low = None
            for l in range(NL):
                ls = pl.ds(l, 1)
                lzv, lev = lights[2, ls, :], lights[3, ls, :]
                dz = lzv - sv
                dist = dz * dz + c2[l, rs, :]
                facing = dz - sxv * dx1[ls, :] - syv * dy1[l, rs, :]
                ri = lax.rsqrt(dist)
                r2 = ri * ri
                fall = lev * (r2 * ri)
                fac = fall * facing
                if it == 0:
                    seen = obs_all[u, l].astype(f32) * ROOT
                    obs_f[u, l] = seen
                else:
                    seen = obs_f[u, l]
                t = av * fac - seen
                tt[l] = t
                ff[l] = fall
                fp[l] = fac
                gg[l] = dz * r2
                uu = t * t
                low = uu if low is None else jnp.minimum(low, uu)
            acc = None
            for l in range(NL):
                ls = pl.ds(l, 1)
                t = tt[l]
                p = jnp.exp2(low - t * t)
                w = p * t
                pull = w * ff[l]
                pf = w * fp[l]
                new = (p, pf, pf * gg[l], pull, pull * dx1[ls, :], pull * dy1[l, rs, :])
                acc = new if acc is None else tuple(a + b for a, b in zip(acc, new))
            ssum, A, D, PU, X, Y = acc
            scale = pix[5, rs, :] / ssum
            alb = alb_own[rs, :]
            ga = scale * A
            ca = scale * alb
            tilt = ga * alb * pix[6, rs, :]
            ga_all[it, rs, own] = ga
            gd[rs, :] = ca * (3.0 * D - PU)
            gx[rs, :] = -ca * X - tilt * sxv
            gypad[pl.ds(pl.multiple_of(u * UNIT + 8, 8), UNIT), :] = -ca * Y - tilt * syv
            return carry

        if it == 0:
            lax.fori_loop(0, nu, unit, 0)
        else:
            lax.fori_loop(0, nu - 1, unit, 0)
            gx_lo, gx_hi = side_gradient(0), side_gradient(1)
            unit(nu - 1, 0)
        lo_v, hi_v = widen(gx[...], gx_lo, gx_hi)
        fd = gd[...] + 0.5 * (lo_v - hi_v) + 0.5 * (gypad[pl.ds(7, rows), :] - gypad[pl.ds(9, rows), :])
        ga = ga_all[it, :, own]
        total = jnp.concatenate(
            [jnp.sum(fd * fd, axis=0, keepdims=True), jnp.sum(ga * ga, axis=0, keepdims=True)], axis=0
        )
        for k, sums in enumerate((near_sums, far_sums)):
            sums[it, pl.ds(slot[k], 1)] = total[None]
            part = sums.at[it, slot[k]]
            for p in phases[k]:
                remote(part, part, ar_send.at[it, k], ar_recv.at[it, k], p).start()
            if k == 0:
                fd_all[it, :, own] = fd
                theirs = pl.ds(pl.multiple_of((q ^ 2) * LANES, LANES), LANES)

                def moves(n, cols, device):
                    return [
                        remote(
                            ref.at[it, :, cols], ref.at[it, :, cols], fd_send.at[it, n, m], fd_recv.at[it, n, m], device
                        )
                        for m, ref in enumerate((fd_all, ga_all))
                    ]

                over, to_mate, onward = moves(0, own, across), moves(1, own, mate), moves(2, theirs, mate)
                if not last:
                    pack_edges(1, ((fd, True), (ga, False)))
                    pk = send_edges(1)
                for c in over + to_mate:
                    c.start()
            else:
                for c in over:
                    c.wait()
                for c in onward:
                    c.start()
                if not last:
                    lax.fori_loop(0, nu, drain, 0)
                if last:
                    for w in sent[:-1]:
                        w.wait_send()
                    for c in gathered:
                        c.wait()
                    depth[...] = depth[...] - step_depth * jnp.tanh(fd_all[0] * inv_d)
                    albedo[...] = albedo[...] - step_albedo * jnp.tanh(ga_all[0] * inv_a)
            whole = sums.at[it, pl.ds(0, counts[k] - 1)]
            w = remote(whole, whole, ar_send.at[it, k], ar_recv.at[it, k], phases[k][0])
            w.wait_recv()
            sent.append(w)
            total = jnp.sum(sums[it], axis=0)
        means = jnp.sum(total, axis=1, keepdims=True) / (rows * float(TOTAL))
        inv = 1.0 / jnp.sqrt(means + epsilon)
        inv_d, inv_a = inv[0:1, 0:1], inv[1:2, 0:1]
        if last:
            for c in to_mate + onward:
                c.wait()
            depth_out[...] = depth[...] - step_depth * jnp.tanh(fd_all[it] * inv_d)
            albedo_out[...] = albedo[...] - step_albedo * jnp.tanh(ga_all[it] * inv_a)
        else:
            gathered = to_mate + onward
            spad[center, :] = spad[center, :] - step_depth * jnp.tanh(fd_all[it, :, own] * inv_d)
            alb_own[...] = alb_own[...] - step_albedo * jnp.tanh(ga_all[it, :, own] * inv_a)
            for c in pk:
                c.wait()
            for side in range(2):
                v = pack_in[1, side]
                halo[side, 0:2, :] = keep[side] * (halo[side, 0:2, :] - step_depth * jnp.tanh(v[0:2] * inv_d))
                halo[side, 2:3, :] = halo[side, 2:3, :] - step_albedo * jnp.tanh(v[2:3] * inv_a)

    for w in sent[-2:]:
        w.wait_send()


def write_out(depth_in, albedo_in, depth_hbm, albedo_hbm, sem):
    copies = [
        pltpu.make_async_copy(depth_in, depth_hbm, sem.at[0]),
        pltpu.make_async_copy(albedo_in, albedo_hbm, sem.at[1]),
    ]
    for c in copies:
        c.start()
    for c in copies:
        c.wait()


def factors(n):
    return {128: (8, 8, 2)}[n]


def solution(mesh):
    NQ, NS = mesh.shape["light"], mesh.shape["strip"]

    def shards(depth, albedo, obs, table, mask):
        rows, cols = depth.shape
        nl = obs.shape[0]
        FACT = factors(NS)
        NL = NQ * nl
        nu = rows // UNIT
        cfg = (NQ, NS, cols, cols * NS, FACT)
        V, D = pltpu.VMEM, pltpu.SemaphoreType.DMA
        any_spec = pl.BlockSpec(memory_space=pl.ANY)
        vm = pl.BlockSpec(memory_space=pltpu.VMEM)
        out = jax.ShapeDtypeStruct((rows, cols), f32)
        results = pl.pallas_call(
            functools.partial(kernel, cfg),
            out_shape=(out, out),
            in_specs=[any_spec] * 3 + [pl.BlockSpec(memory_space=pltpu.SMEM), any_spec],
            out_specs=(vm, vm),
            scratch_shapes=[
                V((rows, cols), f32), V((rows, cols), f32), V((rows, cols), jnp.int32),
                V((nl, rows, cols), jnp.bfloat16), V((nu, NL, UNIT, LANES), jnp.bfloat16),
                V((NQ, 4, LANES), f32), V((4, NL, LANES), f32),
                V((NL, LANES), f32), V((NL, rows, LANES), f32), V((nu, NL, UNIT, LANES), f32),
                V((NL, rows, LANES), f32), V((rows + 16, LANES), f32), V((rows, LANES), f32),
                V((rows, LANES), f32), V((rows + 16, LANES), f32), V((rows, LANES), f32), V((7, rows, LANES), f32),
                V((NL, UNIT, LANES), f32), V((NL, UNIT, LANES), f32),
                V((NL, UNIT, LANES), f32), V((NL, UNIT, LANES), f32),
                V((2 * NQ, nl, LANES), f32), V((2, NL, LANES), f32), V((2, nl, LANES), f32),
                V((ITERS, 2, 8, LANES), f32), V((ITERS, 2, 8, LANES), f32), V((2, 8, LANES), f32),
                V((ITERS, rows, cols), f32), V((ITERS, rows, cols), f32),
                V((ITERS, NQ * FACT[2], 2, LANES), f32), V((ITERS, FACT[0] * FACT[1], 2, LANES), f32),
                D((4,)), D((1,)), D((NQ - 1, nu)), D((NQ - 1, nu)), D((NQ - 1,)), D((NQ - 1,)),
                D((NQ - 1, 2)), D((NQ - 1, 2)), D((2,)), D((2,)),
                D((ITERS, 2)), D((ITERS, 2)), D((ITERS, 3, 2)), D((ITERS, 3, 2)), D((ITERS, 2)), D((ITERS, 2)),
            ],
            compiler_params=pltpu.CompilerParams(
                collective_id=0, has_side_effects=True, vmem_limit_bytes=40 * 2**20
            ),
            cost_estimate=pl.CostEstimate(flops=10**8, bytes_accessed=3 * 2**20, transcendentals=10**6),
            name="steps",
        )(*(pltpu.with_memory_space_constraint(v, pltpu.HBM) for v in (depth, albedo, obs, table.T, mask)))
        return pl.pallas_call(
            write_out,
            out_shape=(out, out),
            in_specs=[vm, vm],
            out_specs=(pl.BlockSpec(memory_space=pltpu.HBM),) * 2,
            scratch_shapes=[D((2,))],
            compiler_params=pltpu.CompilerParams(vmem_limit_bytes=16 * 2**20),
            name="write_out",
        )(*results)

    in_specs = (
        P(None, "strip"),
        P(None, "strip"),
        P("light", None, "strip"),
        P("light", None),
        P(None, "strip"),
    )
    return jax.shard_map(
        shards, mesh=mesh, in_specs=in_specs, out_specs=(P(None, "strip"), P(None, "strip")), check_vma=False
    )
```
